128 devices in a mesh: seq: 16 (over z_lo, x, core), head: 8 (over z_hi, y).
Axes of the slice: x: 4, y: 4, z: 4 (z_hi: 2, z_lo: 2; z = z_hi * 2 + z_lo), core: 2. Of those that a mesh axis runs over, the one named last changes fastest.
Arguments:
- queries: bfloat16 [16384, 2048], P('seq', 'head'), may hold values from -6 to 6
- segment_keys: bfloat16 [16384, 2048], P('seq', 'head'), may hold values from -6 to 6
- segment_values: bfloat16 [16384, 2048], P('seq', 'head'), may hold values from -6 to 6
- memory_keys: bfloat16 [65536, 2048], P('seq', 'head'), may hold values from -8 to 8
- memory_values: bfloat16 [65536, 2048], P('seq', 'head'), may hold values from -6 to 6
- block_index: int32 [64, 8], P('seq'), may hold values from 0 to 1023, as said below
- out_weight: bfloat16 [2048, 4096], P('head'), may hold values from -1.5 to 1.5
Outputs:
- layer_output: bfloat16 [16384, 4096], P('seq', 'head')
The draws below stay inside these ranges and needn't reach their ends.
Inputs may be any that keep to these rules, and one draw needn't show every extreme that they name: `block_index`: from the groups of one index of seq, one memory shard of 64 blocks (the same shard for every index of seq) receives exactly 8 indices, the same 8 distinct blocks from every index; the remaining indices are spread over the other shards as evenly as possible, in a drawn order, so that each of them receives at most 2 from one index, and some receives exactly 2.
All inputs are finite; a program needn't handle non-finite values.
Results may differ from the reference program's by a relative error of at most 0.019.
Values may be sent and summed in bfloat16 or wider, within the bound.
A program may use at most 128 MiB of HBM per device.

```python
import jax
import jax.numpy as jnp
from jax import lax

D = 4096
H = 16
HD = 128
GROUP = 256
BLOCK = 64
TOPB = 8
TOKENS = 16384
MEMORY = 65536
BLK_DEV = 64
BLOCKS = 1024
GROUPS = 64
GROUPS_DEV = 4
SLOTS = 32
CAP = 8


def draw_queries(key, part):
    key = jax.random.fold_in(key, 3)
    base = 1.4 * jax.random.truncated_normal(key, -4.2, 4.2, (TOKENS, H * HD), jnp.float32)
    return base.astype(jnp.bfloat16)


def draw_segment_keys(key, part):
    key = jax.random.fold_in(key, 5)
    base = 1.4 * jax.random.truncated_normal(key, -4.2, 4.2, (TOKENS, H * HD), jnp.float32)
    return base.astype(jnp.bfloat16)


def draw_block_index(key, part):
    key = jax.random.fold_in(key, 7)
    owners_n = GROUPS // GROUPS_DEV
    others_n = owners_n - 1
    key_hot, key_popular, key_devices = jax.random.split(key, 3)
    hot_owner = jax.random.randint(key_hot, (), 0, owners_n)
    popular = jax.random.permutation(key_popular, BLK_DEV)[:CAP]
    ranks = jnp.arange(SLOTS)

    def one_device(device_key):
        key_order, key_spare, key_place = jax.random.split(device_key, 3)
        order = jax.random.permutation(key_order, others_n)
        other_owner = order[(ranks - CAP) % others_n]
        other_owner = other_owner + (other_owner >= hot_owner).astype(jnp.int32)
        spare = jax.random.randint(key_spare, (SLOTS,), 0, BLK_DEV)
        hot_local = popular[jnp.minimum(ranks, CAP - 1)]
        holder = jnp.where(ranks < CAP, hot_owner, other_owner)
        local_block = jnp.where(ranks < CAP, hot_local, spare)
        chosen = holder * BLK_DEV + local_block
        placing = jax.random.permutation(key_place, SLOTS)
        return jnp.take(chosen, placing)
    device_keys = jax.random.split(key_devices, owners_n)
    return jax.vmap(one_device)(device_keys).reshape(GROUPS, TOPB).astype(jnp.int32)


def shard_levels(stream_key, shape, pieces, least, top_value):
    def one(dim, parts):
        heights = jax.random.uniform(jax.random.fold_in(jax.random.fold_in(stream_key, 6), dim), (parts,), jnp.float32, least / len(pieces), top_value / len(pieces))
        return jnp.repeat(jnp.exp(heights), shape[dim] // parts).reshape((-1,) + (1,) * (len(shape) - dim - 1))

    factor_of = one(*pieces[0])
    for cut in pieces[1:]:
        factor_of = factor_of * one(*cut)
    return factor_of


def gaussian(rng, dims, spread, most, pieces=(), held_as=jnp.bfloat16):
    level = shard_levels(rng, dims, pieces, -0.22, 0.18) if pieces else 1.0
    drawn = jax.random.normal(rng, dims, jnp.float32) * spread * level
    return jnp.minimum(jnp.maximum(drawn, -most), most).astype(held_as)


def setup_inputs(seed: int = 0) -> dict:
    key_list = jax.random.split(jax.random.key(seed), 8)
    return {
        "queries": draw_queries(jax.random.fold_in(key_list[7], 71), 0),
        "segment_keys": draw_segment_keys(jax.random.fold_in(key_list[7], 71), 0),
        "segment_values": gaussian(key_list[2], (TOKENS, H * HD), 1.0, 6.0, ((0, 16), (1, 8))),
        "memory_keys": gaussian(key_list[3], (MEMORY, H * HD), 1.4, 8.0, ((0, 16), (1, 8))),
        "memory_values": gaussian(key_list[4], (MEMORY, H * HD), 1.0, 6.0, ((0, 16), (1, 8))),
        "block_index": draw_block_index(jax.random.fold_in(key_list[7], 71), 0),
        "out_weight": gaussian(key_list[6], (H * HD, D), 16 ** -0.5, 1.5, ((0, 8),)),
    }


def reference(queries, segment_keys, segment_values, memory_keys, memory_values, block_index, out_weight):
    score_scale = HD ** -0.5
    key_all = segment_keys.astype(jnp.float32).reshape(TOKENS, H, HD)
    value_all = segment_values.astype(jnp.float32).reshape(TOKENS, H, HD)
    query_groups = queries.astype(jnp.float32).reshape(GROUPS, GROUP, H, HD)
    memory_key_blocks = memory_keys.reshape(BLOCKS, BLOCK, H * HD)
    memory_value_blocks = memory_values.reshape(BLOCKS, BLOCK, H * HD)
    key_positions = jnp.arange(TOKENS, dtype=jnp.int32)

    def one_group(element):
        query_block, chosen, group_number = element
        query_pos = group_number * GROUP + jnp.arange(GROUP, dtype=jnp.int32)
        fetched_keys = jnp.take(memory_key_blocks, chosen, axis=0).reshape(TOPB * BLOCK, H, HD).astype(jnp.float32)
        fetched_values = jnp.take(memory_value_blocks, chosen, axis=0).reshape(TOPB * BLOCK, H, HD).astype(jnp.float32)
        allowed = (key_positions[None, :] <= query_pos[:, None])[None]
        local_scores = jnp.einsum("qhd,khd->hqk", query_block, key_all, precision=lax.Precision.HIGHEST) * score_scale
        local_scores = jnp.where(allowed, local_scores, -jnp.inf)
        memory_scores = jnp.einsum("qhd,khd->hqk", query_block, fetched_keys, precision=lax.Precision.HIGHEST) * score_scale
        row_max = jnp.maximum(jnp.max(local_scores, axis=-1), jnp.max(memory_scores, axis=-1))
        local_weights = jnp.where(allowed, jnp.exp(local_scores - row_max[..., None]), 0.0)
        memory_weights = jnp.exp(memory_scores - row_max[..., None])
        row_sum = jnp.sum(local_weights, axis=-1) + jnp.sum(memory_weights, axis=-1)
        rounded_local = lax.optimization_barrier(local_weights.astype(jnp.bfloat16)).astype(jnp.float32)
        rounded_memory = lax.optimization_barrier(memory_weights.astype(jnp.bfloat16)).astype(jnp.float32)
        numerator = jnp.einsum("hqk,khd->qhd", rounded_local, value_all, precision=lax.Precision.HIGHEST)
        numerator = numerator + jnp.einsum("hqk,khd->qhd", rounded_memory, fetched_values, precision=lax.Precision.HIGHEST)
        result = numerator / jnp.transpose(row_sum)[:, :, None]
        return result.reshape(GROUP, H * HD).astype(jnp.bfloat16)

    attended = lax.map(one_group, (query_groups, block_index, jnp.arange(GROUPS, dtype=jnp.int32)))
    attended = attended.reshape(TOKENS, H * HD)
    return jnp.dot(attended, out_weight, preferred_element_type=jnp.float32).astype(jnp.bfloat16)
```

```python
import functools
import math

import jax
import jax.numpy as jnp
from jax import lax
from jax.experimental import pallas as pl
from jax.experimental.pallas import tpu as pltpu
from jax.sharding import PartitionSpec as P

MESH = pl.DeviceIdType.MESH
HD = 128
GROUP = 256
BLOCK = 64
TOPB = 8
ROWS = 1024
CHUNK = 256
SCALE = math.log2(math.e) / math.sqrt(HD)
LOW = -1e30
STEPS = 24


def where_am_i():
    s = lax.axis_index("seq")
    hd = lax.axis_index("head")
    return s, hd, s // 8, (s // 2) % 4, s % 2, hd // 4, hd % 4


def seq_of(z, x, c):
    return z * 8 + x * 2 + c


def dot_nt(a, b):
    return lax.dot_general(a, b, (((1,), (1,)), ((), ())), preferred_element_type=jnp.float32)


def pick(t, table, default):
    out = default
    for k, v in table.items():
        out = jnp.where(t == k, v, out)
    return out


def remote(src, dst, ss, rs, dev):
    return pltpu.make_async_remote_copy(
        src_ref=src, dst_ref=dst, send_sem=ss, recv_sem=rs, device_id=dev, device_id_type=MESH
    )


DXS = (0, 0, 3, 1, 3, 1, 2, 2)
SIBS = (0, 1, 0, 0, 1, 1, 0, 1)
SERVICE_A = {1: 1, 2: 2, 4: 4, 5: 5, 6: 8, 7: 7, 10: 9, 12: 10, 16: 12, 18: 13, 20: 14, 22: 15}
SERVICE_B = {2: 3, 6: 6, 12: 11}


def attention_kernel(
    q_hbm, k_hbm, v_hbm, mk_hbm, mv_hbm, req_ref, info_ref, w_hbm,
    o_ref, wc_hbm,
    q, kv, m_s, l_s, acc, mk, mv, stage, mem, kc, vc,
    hsend, hown, hr0, hm1, hr1, hm2, hr2, hm3, hr3,
    reqin, infoin, reqs, infos,
    loc_sem, kv_recv, ring_send, swap_send, q_recv, info_recv,
    req_send, req_recv, mem_send, mem_recv, hot_send, hot_recv, w_send, w_recv,
):
    s, hd, z, x, c, zh, y = where_am_i()
    me = s
    zp = seq_of(1 - z, x, c)
    sib = seq_of(z, x, 1 - c)
    xr = seq_of(z, lax.rem(x + 1, 4), c)
    xl = seq_of(z, lax.rem(x + 3, 4), c)

    mine = pl.ds(pl.multiple_of(z * HD, HD), HD)
    theirs = pl.ds(pl.multiple_of((1 - z) * HD, HD), HD)
    loc = [
        pltpu.make_async_copy(k_hbm.at[:, mine], kv.at[s, 0], loc_sem.at[0]),
        pltpu.make_async_copy(v_hbm.at[:, mine], kv.at[s, 1], loc_sem.at[1]),
        pltpu.make_async_copy(q_hbm.at[:, mine], q.at[z], loc_sem.at[2]),
        pltpu.make_async_copy(mk_hbm, mk, loc_sem.at[3]),
        pltpu.make_async_copy(mv_hbm, mv, loc_sem.at[4]),
        pltpu.make_async_copy(info_ref, infos.at[z], loc_sem.at[5]),
        pltpu.make_async_copy(req_ref.at[s], reqin.at[s], loc_sem.at[6]),
    ]
    for cp in loc:
        cp.start()

    bar = pltpu.get_barrier_semaphore()

    def w_target(i):
        same = (i // 4) == zh
        zd = jnp.where(same, z, 1 - z)
        return (seq_of(zd, x, c), i)

    def greet(i, _):
        @pl.when(i != s)
        def _():
            pl.semaphore_signal(bar, inc=1, device_id=(i, hd), device_id_type=MESH)
        return 0

    lax.fori_loop(0, 16, greet, 0)

    def greet_w(i, _):
        @pl.when(i != hd)
        def _():
            pl.semaphore_signal(bar, inc=1, device_id=w_target(i), device_id_type=MESH)
        return 0

    lax.fori_loop(0, 8, greet_w, 0)
    pl.semaphore_wait(bar, 22)

    swaps = [
        remote(k_hbm.at[:, theirs], kv.at[s, 0], swap_send.at[0], kv_recv.at[s * 2], (zp, hd)),
        remote(v_hbm.at[:, theirs], kv.at[s, 1], swap_send.at[1], kv_recv.at[s * 2 + 1], (zp, hd)),
        remote(info_ref, infoin, swap_send.at[2], info_recv.at[0], (zp, hd)),
        remote(q_hbm.at[:, theirs], q.at[z], swap_send.at[3], q_recv.at[0], (zp, hd)),
    ]
    for cp in swaps:
        cp.start()

    def req_copy(i):
        return remote(req_ref.at[i], reqin.at[s], req_send.at[i], req_recv.at[s], (i, hd))

    def send_req(i, _):
        @pl.when(i != s)
        def _():
            req_copy(i).start()
        return 0

    lax.fori_loop(0, 16, send_req, 0)

    loc[0].wait()
    loc[1].wait()

    def ring_copy(half, n, g, k, dev):
        return remote(
            kv.at[g, k], kv.at[g, k], ring_send.at[half * 14 + n], kv_recv.at[g * 2 + k], (dev, hd)
        )

    def sends_of(kind, half, g):
        if kind == 0:
            return [
                ring_copy(half, 0, g, 0, xr), ring_copy(half, 1, g, 0, xl),
                ring_copy(half, 2, g, 1, xr), ring_copy(half, 3, g, 1, xl),
                ring_copy(half, 4, g, 0, sib), ring_copy(half, 5, g, 1, sib),
            ]
        if kind == 2:
            return [
                ring_copy(half, 6, g, 0, xr),
                ring_copy(half, 7, g, 0, sib), ring_copy(half, 8, g, 1, sib),
            ]
        if kind == 3:
            return [
                ring_copy(half, 9, g, 1, xl),
                ring_copy(half, 10, g, 0, sib), ring_copy(half, 11, g, 1, sib),
            ]
        return [ring_copy(half, 12, g, 0, sib), ring_copy(half, 13, g, 1, sib)]

    def block_of(half, i):
        dx = pick(i, dict(enumerate(DXS)), 0)
        sb = pick(i, dict(enumerate(SIBS)), 0)
        return seq_of(half, lax.rem(x + dx, 4), jnp.where(sb == 1, 1 - c, c))

    for cp in sends_of(0, z, s):
        cp.start()

    def w_copy(i):
        cols = pl.ds(pl.multiple_of(i * 512, 512), 512)
        rows = pl.ds(pl.multiple_of(hd * 256, 256), 256)
        return remote(
            w_hbm.at[:, cols], wc_hbm.at[rows, :], w_send.at[i], w_recv.at[hd], w_target(i)
        )

    def send_w(i, _):
        @pl.when(i != hd)
        def _():
            w_copy(i).start()
        return 0

    lax.fori_loop(0, 8, send_w, 0)
    w_local = pltpu.make_async_copy(
        w_hbm.at[:, pl.ds(pl.multiple_of(hd * 512, 512), 512)],
        wc_hbm.at[pl.ds(pl.multiple_of(hd * 256, 256), 256), :],
        loc_sem.at[7],
    )
    w_local.start()

    m_s[...] = jnp.full_like(m_s, LOW)
    l_s[...] = jnp.zeros_like(l_s)
    acc[...] = jnp.zeros_like(acc)

    def wait_block(g):
        for k in range(2):
            remote(kv.at[g, k], kv.at[g, k], ring_send.at[0], kv_recv.at[g * 2 + k], (sib, hd)).wait_recv()

    def service(code):
        @pl.when(code >= 0)
        def _():
            half = jnp.where(code >= 8, 1 - z, z)
            i = lax.rem(code, 8)
            g = block_of(half, i)
            wait_block(g)
            for kind in (0, 2, 3, 6):
                @pl.when(i == kind)
                def _(kind=kind):
                    for cp in sends_of(kind, half, g):
                        cp.start()

    def pipelined(n, scores, finish):
        state = scores(0)
        for j in range(n):
            later = scores(j + 1) if j + 1 < n else None
            finish(j, state)
            state = later

    def absorb(qh, rows, sc, val):
        mo = m_s[qh, rows, :]
        mn = jnp.maximum(mo, jnp.max(sc, axis=-1, keepdims=True))
        m_s[qh, rows, :] = mn
        return sc, mo, mn, val

    def settle(qh, rows, state):
        sc, mo, mn, val = state
        p = jnp.exp2((sc - mn[:, :1]) * SCALE)
        sh = jnp.exp2((mo - mn) * SCALE)
        ls = p[:, 0:128]
        for u in range(1, p.shape[1] // 128):
            ls = ls + p[:, u * 128:(u + 1) * 128]
        l_s[qh, rows, :] = l_s[qh, rows, :] * sh + ls
        acc[qh, rows, :] = acc[qh, rows, :] * sh + jnp.dot(
            p.astype(jnp.bfloat16), val(), preferred_element_type=jnp.float32
        )

    def attend(qh, g):
        gq = seq_of(qh, x, c)

        @pl.when(g < gq)
        def _():
            def scores(j):
                rows = pl.ds(j * CHUNK, CHUNK)
                return absorb(
                    qh, rows, dot_nt(q[qh, rows, :], kv[g, 0, :, :]), lambda: kv[g, 1, :, :]
                )

            pipelined(ROWS // CHUNK, scores, lambda j, st: settle(qh, pl.ds(j * CHUNK, CHUNK), st))

        @pl.when(g == gq)
        def _():
            def scores(j):
                rows = pl.ds(j * CHUNK, CHUNK)
                n = (j + 1) * CHUNK
                sc = dot_nt(q[qh, rows, :], kv[g, 0, 0:n, :])
                last = sc[:, n - CHUNK:]
                ok = lax.broadcasted_iota(jnp.int32, (CHUNK, CHUNK), 1) <= lax.broadcasted_iota(
                    jnp.int32, (CHUNK, CHUNK), 0
                )
                last = jnp.where(ok, last, LOW)
                if j:
                    last = jnp.concatenate([sc[:, : n - CHUNK], last], axis=1)
                return absorb(qh, rows, last, lambda: kv[g, 1, 0:n, :])

            pipelined(ROWS // CHUNK, scores, lambda j, st: settle(qh, pl.ds(j * CHUNK, CHUNK), st))

    def mem_copy(r, e):
        dst = seq_of(e, (r // 2) % 4, lax.rem(r, 2))
        at = (r // 8) * 16 + s
        return dst, at

    def pair(at):
        return mem.at[pl.ds(at * 2, 2)]

    def mem_remote(r, e):
        dst, at = mem_copy(r, e)
        return remote(
            stage.at[r, e], pair(at), mem_send.at[r * 2 + e], mem_recv.at[at], (dst, hd)
        )

    def hot_copy(n, src, dst, dev):
        return remote(src, dst, hot_send.at[n], hot_recv.at[n], (dev, hd))

    hx1 = seq_of(z, jnp.where(x % 2 == 0, x + 1, x - 1), c)
    hx2 = seq_of(z, 3 - x, c)

    def hot_copies(n):
        if n == 0:
            return hot_copy(0, hsend, hr0, sib)
        if n == 1:
            return hot_copy(1, hm1.at[1 - z], hr1, zp)
        if n == 2:
            return hot_copy(2, hm2, hr2, hx1)
        if n == 3:
            return hot_copy(3, hm3, hr3, hx2)
        return hot_copy(4, mem.at[pl.ds(64, 8), c], mem.at[pl.ds(64, 8), c], sib)

    def hot_owner():
        return infos[z, 0, 40]

    def step(t, _):
        @pl.when(t == 8)
        def _():
            remote(q.at[0], q.at[1 - z], swap_send.at[3], q_recv.at[0], (zp, hd)).wait_recv()

        service(pick(t, SERVICE_A, -1))
        service(pick(t, SERVICE_B, -1))

        @pl.when(t == 1)
        def _():
            def wait_req(i, _):
                @pl.when(i != s)
                def _():
                    remote(
                        req_ref.at[i], reqin.at[i], req_send.at[i], req_recv.at[i], (sib, hd)
                    ).wait_recv()
                return 0

            lax.fori_loop(0, 16, wait_req, 0)
            swaps[2].wait_recv()
            for cp in loc[3:]:
                cp.wait()
            a = pltpu.make_async_copy(reqin, reqs, loc_sem.at[8])
            b = pltpu.make_async_copy(infoin, infos.at[1 - z], loc_sem.at[9])
            a.start()
            b.start()
            a.wait()
            b.wait()

            def hot_rows(j, _):
                b = infos[z, 0, 32 + j]
                kr = mk[b]
                vr = mv[b]
                for e in range(2):
                    cols = slice(e * HD, (e + 1) * HD)
                    hown[e, j] = jnp.where(c == 0, kr[:, cols], vr[:, cols])
                    hsend[e, j] = jnp.where(c == 0, vr[:, cols], kr[:, cols])
                return 0

            lax.fori_loop(0, 8, hot_rows, 0)
            hot_copies(0).start()

            def gather(r, _):
                for b2 in range(2):
                    b = reqs[r, 0, b2]
                    kr = mk[b]
                    vr = mv[b]
                    for e in range(2):
                        cols = slice(e * HD, (e + 1) * HD)
                        stage[r, e, b2, 0] = kr[:, cols]
                        stage[r, e, b2, 1] = vr[:, cols]
                return 0

            lax.fori_loop(0, 16, gather, 0)

        @pl.when(t == 4)
        def _():
            hot_copies(0).wait_recv()
            keep = hot_owner() == me
            hm1[...] = jnp.where(keep, hown[...], hr0[...])
            hot_copies(1).start()

        @pl.when(t == 6)
        def _():
            def send(i, _):
                r = lax.rem(i // 2 + s + 1, 16)
                e = lax.rem(i, 2)
                dst, at = mem_copy(r, e)

                @pl.when(dst == s)
                def _():
                    pltpu.make_async_copy(stage.at[r, e], pair(at), mem_recv.at[at]).start()

                @pl.when(dst != s)
                def _():
                    mem_remote(r, e).start()
                return 0

            lax.fori_loop(0, 32, send, 0)

        @pl.when(t == 7)
        def _():
            hot_copies(1).wait_recv()
            keep = (hot_owner() // 8) == z
            hm2[...] = jnp.where(keep, hm1[z], hr1[...])
            hot_copies(2).start()

        @pl.when(t == 11)
        def _():
            hot_copies(2).wait_recv()
            keep = ((hot_owner() // 2) % 4) == x
            hm3[...] = jnp.where(keep, hm2[...], hr2[...])
            hot_copies(3).start()

        @pl.when(t == 14)
        def _():
            hot_copies(3).wait_recv()
            keep = ((hot_owner() // 4) % 2) == (x // 2)
            for j in range(8):
                mem[64 + j, c] = jnp.where(keep, hm3[j], hr3[j])
            hot_copies(4).start()

        native = t < 8
        u = t - 8
        qh = jnp.where(native, z, jnp.where(z == 0, 1, lax.rem(t, 2)))
        half = jnp.where(native, z, jnp.where((z == 0) & (u >= 8), 1, 0))
        i = jnp.where(native, t, jnp.where(z == 0, lax.rem(t, 8), u // 2))
        attend(qh, block_of(half, i))
        return 0

    loc[2].wait()
    lax.fori_loop(0, STEPS, step, 0)

    def wait_mem(i, _):
        o = lax.rem(i, 16)

        @pl.when(o != s)
        def _():
            remote(stage.at[0, 0], pair(i), mem_send.at[0], mem_recv.at[i], (sib, hd)).wait_recv()

        @pl.when(o == s)
        def _():
            pltpu.make_async_copy(stage.at[0, 0], pair(i), mem_recv.at[i]).wait()
        return 0

    lax.fori_loop(0, 32, wait_mem, 0)
    remote(
        mem.at[pl.ds(64, 8), 0], mem.at[pl.ds(64, 8), 1 - c], hot_send.at[4], hot_recv.at[4], (sib, hd)
    ).wait_recv()

    def mem_group(i, _):
        qh = i // 4
        j = lax.rem(i, 4)
        for e in range(TOPB):
            code = infos[qh, 0, j * TOPB + e]
            kc[e * BLOCK:(e + 1) * BLOCK, :] = mem[code, 0]
            vc[e * BLOCK:(e + 1) * BLOCK, :] = mem[code, 1]
        rows = pl.ds(pl.multiple_of(j * GROUP, GROUP), GROUP)
        st = absorb(qh, rows, dot_nt(q[qh, rows, :], kc[...]), lambda: vc[...])
        settle(qh, rows, st)
        o_ref[qh, rows, :] = (
            acc[qh, rows, :] / jnp.sum(l_s[qh, rows, :], axis=-1, keepdims=True)
        ).astype(jnp.bfloat16)
        return 0

    lax.fori_loop(0, 8, mem_group, 0)

    for cp in swaps:
        cp.wait_send()
    for half in (0, 1):
        for kind in (0, 2, 3, 6):
            for cp in sends_of(kind, half, s):
                cp.wait_send()
    for n in range(5):
        hot_copies(n).wait_send()

    def drain_req(i, _):
        @pl.when(i != s)
        def _():
            req_copy(i).wait_send()
        return 0

    lax.fori_loop(0, 16, drain_req, 0)

    def drain_mem(i, _):
        dst, _at = mem_copy(i // 2, lax.rem(i, 2))

        @pl.when(dst != s)
        def _():
            mem_remote(i // 2, lax.rem(i, 2)).wait_send()
        return 0

    lax.fori_loop(0, 32, drain_mem, 0)

    def drain_w(i, _):
        @pl.when(i != hd)
        def _():
            w_copy(i).wait_send()
            rows = pl.ds(pl.multiple_of(i * 256, 256), 256)
            remote(
                w_hbm.at[:, pl.ds(0, 512)], wc_hbm.at[rows, :], w_send.at[i], w_recv.at[i], (sib, hd)
            ).wait_recv()
        return 0

    lax.fori_loop(0, 8, drain_w, 0)
    w_local.wait()


def attention(q, k, v, mk, mv, req, info, w):
    any_ = pl.BlockSpec(memory_space=pl.ANY)
    vm = pl.BlockSpec(memory_space=pltpu.VMEM)
    b16 = jnp.bfloat16
    hot = (8, BLOCK, HD)
    dma = pltpu.SemaphoreType.DMA
    return pl.pallas_call(
        attention_kernel,
        out_shape=(
            jax.ShapeDtypeStruct((2, ROWS, HD), b16),
            jax.ShapeDtypeStruct((2048, 512), b16),
        ),
        in_specs=[any_] * 5 + [vm, vm, any_],
        out_specs=(vm, any_),
        scratch_shapes=[
            pltpu.VMEM((2, ROWS, HD), b16),
            pltpu.VMEM((16, 2, ROWS, HD), b16),
            pltpu.VMEM((2, ROWS, HD), jnp.float32),
            pltpu.VMEM((2, ROWS, HD), jnp.float32),
            pltpu.VMEM((2, ROWS, HD), jnp.float32),
            pltpu.VMEM((64, BLOCK, 2 * HD), b16),
            pltpu.VMEM((64, BLOCK, 2 * HD), b16),
            pltpu.VMEM((16, 2, 2, 2, BLOCK, HD), b16),
            pltpu.VMEM((72, 2, BLOCK, HD), b16),
            pltpu.VMEM((TOPB * BLOCK, HD), b16),
            pltpu.VMEM((TOPB * BLOCK, HD), b16),
            pltpu.VMEM((2,) + hot, b16),
            pltpu.VMEM((2,) + hot, b16),
            pltpu.VMEM((2,) + hot, b16),
            pltpu.VMEM((2,) + hot, b16),
            pltpu.VMEM(hot, b16),
            pltpu.VMEM(hot, b16),
            pltpu.VMEM(hot, b16),
            pltpu.VMEM(hot, b16),
            pltpu.VMEM(hot, b16),
            pltpu.VMEM((16, 8, 128), jnp.int32),
            pltpu.VMEM((8, 128), jnp.int32),
            pltpu.SMEM((16, 8, 128), jnp.int32),
            pltpu.SMEM((2, 8, 128), jnp.int32),
            dma((10,)),
            dma((32,)),
            dma((28,)),
            dma((4,)),
            dma((1,)),
            dma((1,)),
            dma((16,)),
            dma((16,)),
            dma((32,)),
            dma((32,)),
            dma((5,)),
            dma((5,)),
            dma((8,)),
            dma((8,)),
        ],
        compiler_params=pltpu.CompilerParams(
            collective_id=0, has_side_effects=True, vmem_limit_bytes=56 << 20
        ),
        name="attention",
    )(q, k, v, mk, mv, req, info, w)


def gather_kernel(o_ref, a_ref, send, recv, ysend, yrecv, loc_sem):
    s, hd, z, x, c, zh, y = where_am_i()
    up = zh * 4 + lax.rem(y + 1, 4)
    dn = zh * 4 + lax.rem(y + 3, 4)
    peers = [(1 - z, zh), (1 - z, 1 - zh), (z, 1 - zh)]
    bar = pltpu.get_barrier_semaphore()
    for zd, zhd in peers:
        pl.semaphore_signal(
            bar, inc=1, device_id=(seq_of(zd, x, c), zhd * 4 + y), device_id_type=MESH
        )
    pl.semaphore_signal(bar, inc=1, device_id=(s, up), device_id_type=MESH)
    pl.semaphore_signal(bar, inc=1, device_id=(s, dn), device_id_type=MESH)
    pl.semaphore_wait(bar, 5)

    def head_cols(zhs, zs):
        return pl.ds(pl.multiple_of(((zhs * 4 + y) * 2 + zs) * HD, HD), HD)

    own = pltpu.make_async_copy(o_ref.at[z], a_ref.at[:, head_cols(zh, z)], loc_sem.at[0])
    own.start()
    outs = []
    for n, (zd, zhd) in enumerate(peers):
        cp = remote(
            o_ref.at[zd], a_ref.at[:, head_cols(zh, z)], send.at[n], recv.at[n],
            (seq_of(zd, x, c), zhd * 4 + y),
        )
        cp.start()
        outs.append(cp)
    own.wait()
    for n, (zd, zhd) in enumerate(peers):
        remote(
            o_ref.at[0], a_ref.at[:, head_cols(zhd, zd)], send.at[n], recv.at[n], (s, hd)
        ).wait_recv()

    def slab(zz, yy):
        return a_ref.at[:, pl.ds(pl.multiple_of((zz * 4 + yy) * 256, 256), 256)]

    def y_copy(n, zz, yy, dev):
        return remote(slab(zz, yy), slab(zz, yy), ysend.at[n], yrecv.at[yy * 2 + zz], (s, dev))

    y1 = lax.rem(y + 3, 4)
    y2 = lax.rem(y + 1, 4)
    y3 = lax.rem(y + 2, 4)
    sends = [y_copy(0, 0, y, up), y_copy(1, 1, y, dn), y_copy(2, 1, y, up), y_copy(3, 0, y, dn)]
    for cp in sends:
        cp.start()
    y_copy(0, 0, y1, up).wait_recv()
    f0 = y_copy(4, 0, y1, up)
    f0.start()
    y_copy(0, 1, y2, up).wait_recv()
    f1 = y_copy(5, 1, y2, dn)
    f1.start()
    for zz, yy in ((1, y1), (0, y2), (0, y3), (1, y3)):
        y_copy(0, zz, yy, up).wait_recv()
    for cp in outs + sends + [f0, f1]:
        cp.wait_send()


def gather(o):
    dma = pltpu.SemaphoreType.DMA
    vm = pl.BlockSpec(memory_space=pltpu.VMEM)
    return pl.pallas_call(
        gather_kernel,
        out_shape=jax.ShapeDtypeStruct((ROWS, 2048), jnp.bfloat16),
        in_specs=[vm],
        out_specs=vm,
        scratch_shapes=[dma((3,)), dma((3,)), dma((6,)), dma((8,)), dma((1,))],
        compiler_params=pltpu.CompilerParams(
            collective_id=1, has_side_effects=True, vmem_limit_bytes=32 << 20
        ),
        name="gather_heads",
    )(o)


def tables(block_index):
    z = lax.axis_index("seq") // 8
    w = block_index.reshape(-1)
    holder = w // 64
    local = w - holder * 64
    owners = jnp.arange(16, dtype=jnp.int32)
    n = jnp.arange(32, dtype=jnp.int32)
    same = holder[:, None] == holder[None, :]
    count = jnp.sum(same.astype(jnp.int32), axis=1)
    place = jnp.sum((same & (n[None, :] < n[:, None])).astype(jnp.int32), axis=1)
    is_hot = count == TOPB
    rank = jnp.sum((same & (local[None, :] < local[:, None])).astype(jnp.int32), axis=1)
    lanes = jnp.arange(128, dtype=jnp.int32)
    hit = (holder[:, None, None] == owners[None, :, None]) & (
        place[:, None, None] == lanes[None, None, :]
    ) & (lanes < 2)[None, None, :]
    req = jnp.sum(jnp.where(hit, local[:, None, None], 0), axis=0)
    code = jnp.where(is_hot, 64 + rank, (z * 16 + holder) * 2 + place)
    at_code = n[:, None] == lanes[None, :]
    at_hot = is_hot[:, None] & ((rank + 32)[:, None] == lanes[None, :])
    at_owner = (is_hot & (rank == 0))[:, None] & (lanes == 40)[None, :]
    info = jnp.sum(
        jnp.where(at_code, code[:, None], 0)
        + jnp.where(at_hot, local[:, None], 0)
        + jnp.where(at_owner, holder[:, None], 0),
        axis=0,
    )
    return (
        jnp.broadcast_to(req[:, None, :], (16, 8, 128)),
        jnp.broadcast_to(info[None, :], (8, 128)),
    )


def shards(q, k, v, mk, mv, block_index, w):
    req, info = tables(block_index)
    o, wc = attention(
        q, k, v, mk.reshape(-1, BLOCK, 2 * HD), mv.reshape(-1, BLOCK, 2 * HD), req, info, w
    )
    a = gather(o)
    return jnp.dot(a, wc, preferred_element_type=jnp.float32).astype(jnp.bfloat16)


def solution(mesh):
    return jax.shard_map(
        shards,
        mesh=mesh,
        in_specs=(
            P("seq", "head"), P("seq", "head"), P("seq", "head"), P("seq", "head"),
            P("seq", "head"), P("seq", None), P("head", None),
        ),
        out_specs=P("seq", "head"),
        check_vma=False,
    )
```

```python
import functools
import math

import jax
import jax.numpy as jnp
from jax import lax
from jax.experimental import pallas as pl
from jax.experimental.pallas import tpu as pltpu
from jax.sharding import PartitionSpec as P

MESH = pl.DeviceIdType.MESH
HD = 128
GROUP = 256
BLOCK = 64
TOPB = 8
ROWS = 1024
CHUNK = 256
SCALE = math.log2(math.e) / math.sqrt(HD)
LOW = -1e30
STEPS = 24
MEM_NEAR = 12
MEM_FAR = 13


def where_am_i():
    s = lax.axis_index("seq")
    hd = lax.axis_index("head")
    return s, hd, s // 8, (s // 2) % 4, s % 2, hd // 4, hd % 4


def seq_of(z, x, c):
    return z * 8 + x * 2 + c


def dot_nt(a, b):
    return lax.dot_general(a, b, (((1,), (1,)), ((), ())), preferred_element_type=jnp.float32)


def pick(t, table, default):
    out = default
    for k, v in table.items():
        out = jnp.where(t == k, v, out)
    return out


def remote(src, dst, ss, rs, dev):
    return pltpu.make_async_remote_copy(
        src_ref=src, dst_ref=dst, send_sem=ss, recv_sem=rs, device_id=dev, device_id_type=MESH
    )


DXS = (0, 0, 3, 1, 3, 1, 2, 2)
SIBS = (0, 1, 0, 0, 1, 1, 0, 1)
SERVICE_A = {1: 1, 2: 2, 4: 4, 5: 5, 6: 8, 7: 7, 10: 9, 12: 10, 16: 12, 18: 13, 20: 14, 22: 15}
SERVICE_B = {2: 3, 6: 6, 12: 11}


def attention_kernel(
    q_hbm, k_hbm, v_hbm, mk_hbm, mv_hbm, req_ref, info_ref, w_hbm,
    o_ref, wc_hbm,
    q, kv, m_s, l_s, acc, mk, mv, stage, mem, kc, vc,
    hsend, hown, hr0, hm1, hr1, hm2, hr2, hm3, hr3,
    reqin, infoin, reqs, infos,
    loc_sem, kv_recv, ring_send, swap_send, q_recv, info_recv,
    req_send, req_recv, mem_send, mem_recv, hot_send, hot_recv, w_send, w_recv,
):
    s, hd, z, x, c, zh, y = where_am_i()
    me = s
    zp = seq_of(1 - z, x, c)
    sib = seq_of(z, x, 1 - c)
    xr = seq_of(z, lax.rem(x + 1, 4), c)
    xl = seq_of(z, lax.rem(x + 3, 4), c)

    mine = pl.ds(pl.multiple_of(z * HD, HD), HD)
    theirs = pl.ds(pl.multiple_of((1 - z) * HD, HD), HD)
    loc = [
        pltpu.make_async_copy(k_hbm.at[:, mine], kv.at[s, 0], loc_sem.at[0]),
        pltpu.make_async_copy(v_hbm.at[:, mine], kv.at[s, 1], loc_sem.at[1]),
        pltpu.make_async_copy(q_hbm.at[:, mine], q.at[z], loc_sem.at[2]),
        pltpu.make_async_copy(mk_hbm, mk, loc_sem.at[3]),
        pltpu.make_async_copy(mv_hbm, mv, loc_sem.at[4]),
        pltpu.make_async_copy(info_ref, infos.at[z], loc_sem.at[5]),
        pltpu.make_async_copy(req_ref.at[s], reqin.at[s], loc_sem.at[6]),
    ]
    for cp in loc:
        cp.start()

    bar = pltpu.get_barrier_semaphore()

    def w_target(i):
        same = (i // 4) == zh
        zd = jnp.where(same, z, 1 - z)
        return (seq_of(zd, x, c), i)

    def greet(i, _):
        @pl.when(i != s)
        def _():
            pl.semaphore_signal(bar, inc=1, device_id=(i, hd), device_id_type=MESH)
        return 0

    lax.fori_loop(0, 16, greet, 0)

    def greet_w(i, _):
        @pl.when(i != hd)
        def _():
            pl.semaphore_signal(bar, inc=1, device_id=w_target(i), device_id_type=MESH)
        return 0

    lax.fori_loop(0, 8, greet_w, 0)
    pl.semaphore_wait(bar, 22)

    swaps = [
        remote(k_hbm.at[:, theirs], kv.at[s, 0], swap_send.at[0], kv_recv.at[s * 2], (zp, hd)),
        remote(v_hbm.at[:, theirs], kv.at[s, 1], swap_send.at[1], kv_recv.at[s * 2 + 1], (zp, hd)),
        remote(info_ref, infoin, swap_send.at[2], info_recv.at[0], (zp, hd)),
        remote(q_hbm.at[:, theirs], q.at[z], swap_send.at[3], q_recv.at[0], (zp, hd)),
    ]
    swaps[2].start()

    def req_copy(i):
        return remote(req_ref.at[i], reqin.at[s], req_send.at[i], req_recv.at[s], (i, hd))

    def send_req(i, _):
        @pl.when(i != s)
        def _():
            req_copy(i).start()
        return 0

    lax.fori_loop(0, 16, send_req, 0)
    swaps[0].start()
    swaps[1].start()

    loc[0].wait()
    loc[1].wait()

    def ring_copy(half, n, g, k, dev):
        return remote(
            kv.at[g, k], kv.at[g, k], ring_send.at[half * 14 + n], kv_recv.at[g * 2 + k], (dev, hd)
        )

    def sends_of(kind, half, g):
        if kind == 0:
            return [
                ring_copy(half, 0, g, 0, xr), ring_copy(half, 1, g, 0, xl),
                ring_copy(half, 2, g, 1, xr), ring_copy(half, 3, g, 1, xl),
                ring_copy(half, 4, g, 0, sib), ring_copy(half, 5, g, 1, sib),
            ]
        if kind == 2:
            return [
                ring_copy(half, 6, g, 0, xr),
                ring_copy(half, 7, g, 0, sib), ring_copy(half, 8, g, 1, sib),
            ]
        if kind == 3:
            return [
                ring_copy(half, 9, g, 1, xl),
                ring_copy(half, 10, g, 0, sib), ring_copy(half, 11, g, 1, sib),
            ]
        return [ring_copy(half, 12, g, 0, sib), ring_copy(half, 13, g, 1, sib)]

    def block_of(half, i):
        dx = pick(i, dict(enumerate(DXS)), 0)
        sb = pick(i, dict(enumerate(SIBS)), 0)
        return seq_of(half, lax.rem(x + dx, 4), jnp.where(sb == 1, 1 - c, c))

    for cp in sends_of(0, z, s):
        cp.start()
    swaps[3].start()

    def w_copy(i):
        cols = pl.ds(pl.multiple_of(i * 512, 512), 512)
        rows = pl.ds(pl.multiple_of(hd * 256, 256), 256)
        return remote(
            w_hbm.at[:, cols], wc_hbm.at[rows, :], w_send.at[i], w_recv.at[hd], w_target(i)
        )

    def send_w(i, _):
        @pl.when(i != hd)
        def _():
            w_copy(i).start()
        return 0

    lax.fori_loop(0, 8, send_w, 0)
    w_local = pltpu.make_async_copy(
        w_hbm.at[:, pl.ds(pl.multiple_of(hd * 512, 512), 512)],
        wc_hbm.at[pl.ds(pl.multiple_of(hd * 256, 256), 256), :],
        loc_sem.at[7],
    )
    w_local.start()

    m_s[...] = jnp.full_like(m_s, LOW)
    l_s[...] = jnp.zeros_like(l_s)
    acc[...] = jnp.zeros_like(acc)

    def wait_block(g):
        for k in range(2):
            remote(kv.at[g, k], kv.at[g, k], ring_send.at[0], kv_recv.at[g * 2 + k], (sib, hd)).wait_recv()

    def service(code):
        @pl.when(code >= 0)
        def _():
            half = jnp.where(code >= 8, 1 - z, z)
            i = lax.rem(code, 8)
            g = block_of(half, i)
            wait_block(g)
            for kind in (0, 2, 3, 6):
                @pl.when(i == kind)
                def _(kind=kind):
                    for cp in sends_of(kind, half, g):
                        cp.start()

    def pipelined(n, scores, finish):
        state = scores(0)
        for j in range(n):
            later = scores(j + 1) if j + 1 < n else None
            finish(j, state)
            state = later

    def absorb(qh, rows, sc, val):
        mo = m_s[qh, rows, :]
        mn = jnp.maximum(mo, jnp.max(sc, axis=-1, keepdims=True))
        m_s[qh, rows, :] = mn
        return sc, mo, mn, val

    def settle(qh, rows, state):
        sc, mo, mn, val = state
        p = jnp.exp2((sc - mn[:, :1]) * SCALE)
        sh = jnp.exp2((mo - mn) * SCALE)
        ls = p[:, 0:128]
        for u in range(1, p.shape[1] // 128):
            ls = ls + p[:, u * 128:(u + 1) * 128]
        l_s[qh, rows, :] = l_s[qh, rows, :] * sh + ls
        acc[qh, rows, :] = acc[qh, rows, :] * sh + jnp.dot(
            p.astype(jnp.bfloat16), val(), preferred_element_type=jnp.float32
        )

    def attend(qh, g):
        gq = seq_of(qh, x, c)

        @pl.when(g < gq)
        def _():
            def scores(j):
                rows = pl.ds(j * CHUNK, CHUNK)
                return absorb(
                    qh, rows, dot_nt(q[qh, rows, :], kv[g, 0, :, :]), lambda: kv[g, 1, :, :]
                )

            pipelined(ROWS // CHUNK, scores, lambda j, st: settle(qh, pl.ds(j * CHUNK, CHUNK), st))

        @pl.when(g == gq)
        def _():
            def scores(j):
                rows = pl.ds(j * CHUNK, CHUNK)
                n = (j + 1) * CHUNK
                sc = dot_nt(q[qh, rows, :], kv[g, 0, 0:n, :])
                last = sc[:, n - CHUNK:]
                ok = lax.broadcasted_iota(jnp.int32, (CHUNK, CHUNK), 1) <= lax.broadcasted_iota(
                    jnp.int32, (CHUNK, CHUNK), 0
                )
                last = jnp.where(ok, last, LOW)
                if j:
                    last = jnp.concatenate([sc[:, : n - CHUNK], last], axis=1)
                return absorb(qh, rows, last, lambda: kv[g, 1, 0:n, :])

            pipelined(ROWS // CHUNK, scores, lambda j, st: settle(qh, pl.ds(j * CHUNK, CHUNK), st))

    def mem_copy(r, e):
        dst = seq_of(e, (r // 2) % 4, lax.rem(r, 2))
        at = (r // 8) * 16 + s
        return dst, at

    def pair(at):
        return mem.at[pl.ds(at * 2, 2)]

    def mem_remote(r, e):
        dst, at = mem_copy(r, e)
        return remote(
            stage.at[r, e], pair(at), mem_send.at[r * 2 + e], mem_recv.at[at], (dst, hd)
        )

    def hot_copy(n, src, dst, dev):
        return remote(src, dst, hot_send.at[n], hot_recv.at[n], (dev, hd))

    hx1 = seq_of(z, jnp.where(x % 2 == 0, x + 1, x - 1), c)
    hx2 = seq_of(z, 3 - x, c)

    def hot_copies(n):
        if n == 0:
            return hot_copy(0, hsend, hr0, sib)
        if n == 1:
            return hot_copy(1, hm1.at[1 - z], hr1, zp)
        if n == 2:
            return hot_copy(2, hm2, hr2, hx1)
        if n == 3:
            return hot_copy(3, hm3, hr3, hx2)
        return hot_copy(4, mem.at[pl.ds(64, 8), c], mem.at[pl.ds(64, 8), c], sib)

    def hot_owner():
        return infos[z, 0, 40]

    def step(t, _):
        @pl.when(t == 8)
        def _():
            remote(q.at[0], q.at[1 - z], swap_send.at[3], q_recv.at[0], (zp, hd)).wait_recv()

        service(pick(t, SERVICE_A, -1))
        service(pick(t, SERVICE_B, -1))

        @pl.when(t == 1)
        def _():
            def wait_req(i, _):
                @pl.when(i != s)
                def _():
                    remote(
                        req_ref.at[i], reqin.at[i], req_send.at[i], req_recv.at[i], (sib, hd)
                    ).wait_recv()
                return 0

            lax.fori_loop(0, 16, wait_req, 0)
            swaps[2].wait_recv()
            for cp in loc[3:]:
                cp.wait()
            a = pltpu.make_async_copy(reqin, reqs, loc_sem.at[8])
            b = pltpu.make_async_copy(infoin, infos.at[1 - z], loc_sem.at[9])
            a.start()
            b.start()
            a.wait()
            b.wait()

            def hot_rows(j, _):
                b = infos[z, 0, 32 + j]
                kr = mk[b]
                vr = mv[b]
                for e in range(2):
                    cols = slice(e * HD, (e + 1) * HD)
                    hown[e, j] = jnp.where(c == 0, kr[:, cols], vr[:, cols])
                    hsend[e, j] = jnp.where(c == 0, vr[:, cols], kr[:, cols])
                return 0

            lax.fori_loop(0, 8, hot_rows, 0)
            hot_copies(0).start()

            def gather(r, _):
                for b2 in range(2):
                    b = reqs[r, 0, b2]
                    kr = mk[b]
                    vr = mv[b]
                    for e in range(2):
                        cols = slice(e * HD, (e + 1) * HD)
                        stage[r, e, b2, 0] = kr[:, cols]
                        stage[r, e, b2, 1] = vr[:, cols]
                return 0

            lax.fori_loop(0, 16, gather, 0)

        @pl.when(t == 4)
        def _():
            hot_copies(0).wait_recv()
            keep = hot_owner() == me
            hm1[...] = jnp.where(keep, hown[...], hr0[...])
            hot_copies(1).start()

        @pl.when((t == MEM_NEAR) | (t == MEM_FAR))
        def _():
            def send(i, _):
                r = lax.rem(i + s + 1, 16)
                e = jnp.where(t == MEM_NEAR, z, 1 - z)
                dst, at = mem_copy(r, e)

                @pl.when(dst == s)
                def _():
                    pltpu.make_async_copy(stage.at[r, e], pair(at), mem_recv.at[at]).start()

                @pl.when(dst != s)
                def _():
                    mem_remote(r, e).start()
                return 0

            lax.fori_loop(0, 16, send, 0)

        @pl.when(t == 7)
        def _():
            hot_copies(1).wait_recv()
            keep = (hot_owner() // 8) == z
            hm2[...] = jnp.where(keep, hm1[z], hr1[...])
            hot_copies(2).start()

        @pl.when(t == 11)
        def _():
            hot_copies(2).wait_recv()
            keep = ((hot_owner() // 2) % 4) == x
            hm3[...] = jnp.where(keep, hm2[...], hr2[...])
            hot_copies(3).start()

        @pl.when(t == 14)
        def _():
            hot_copies(3).wait_recv()
            keep = ((hot_owner() // 4) % 2) == (x // 2)
            for j in range(8):
                mem[64 + j, c] = jnp.where(keep, hm3[j], hr3[j])
            hot_copies(4).start()

        native = t < 8
        u = t - 8
        qh = jnp.where(native, z, jnp.where(z == 0, 1, lax.rem(t, 2)))
        half = jnp.where(native, z, jnp.where((z == 0) & (u >= 8), 1, 0))
        i = jnp.where(native, t, jnp.where(z == 0, lax.rem(t, 8), u // 2))
        attend(qh, block_of(half, i))
        return 0

    loc[2].wait()
    lax.fori_loop(0, STEPS, step, 0)

    def wait_mem(i, _):
        o = lax.rem(i, 16)

        @pl.when(o != s)
        def _():
            remote(stage.at[0, 0], pair(i), mem_send.at[0], mem_recv.at[i], (sib, hd)).wait_recv()

        @pl.when(o == s)
        def _():
            pltpu.make_async_copy(stage.at[0, 0], pair(i), mem_recv.at[i]).wait()
        return 0

    lax.fori_loop(0, 32, wait_mem, 0)
    remote(
        mem.at[pl.ds(64, 8), 0], mem.at[pl.ds(64, 8), 1 - c], hot_send.at[4], hot_recv.at[4], (sib, hd)
    ).wait_recv()

    def mem_group(i, _):
        qh = i // 4
        j = lax.rem(i, 4)
        for e in range(TOPB):
            code = infos[qh, 0, j * TOPB + e]
            kc[e * BLOCK:(e + 1) * BLOCK, :] = mem[code, 0]
            vc[e * BLOCK:(e + 1) * BLOCK, :] = mem[code, 1]
        rows = pl.ds(pl.multiple_of(j * GROUP, GROUP), GROUP)
        st = absorb(qh, rows, dot_nt(q[qh, rows, :], kc[...]), lambda: vc[...])
        settle(qh, rows, st)
        o_ref[qh, rows, :] = (
            acc[qh, rows, :] / jnp.sum(l_s[qh, rows, :], axis=-1, keepdims=True)
        ).astype(jnp.bfloat16)
        return 0

    lax.fori_loop(0, 8, mem_group, 0)

    for cp in swaps:
        cp.wait_send()
    for half in (0, 1):
        for kind in (0, 2, 3, 6):
            for cp in sends_of(kind, half, s):
                cp.wait_send()
    for n in range(5):
        hot_copies(n).wait_send()

    def drain_req(i, _):
        @pl.when(i != s)
        def _():
            req_copy(i).wait_send()
        return 0

    lax.fori_loop(0, 16, drain_req, 0)

    def drain_mem(i, _):
        dst, _at = mem_copy(i // 2, lax.rem(i, 2))

        @pl.when(dst != s)
        def _():
            mem_remote(i // 2, lax.rem(i, 2)).wait_send()
        return 0

    lax.fori_loop(0, 32, drain_mem, 0)

    def drain_w(i, _):
        @pl.when(i != hd)
        def _():
            w_copy(i).wait_send()
            rows = pl.ds(pl.multiple_of(i * 256, 256), 256)
            remote(
                w_hbm.at[:, pl.ds(0, 512)], wc_hbm.at[rows, :], w_send.at[i], w_recv.at[i], (sib, hd)
            ).wait_recv()
        return 0

    lax.fori_loop(0, 8, drain_w, 0)
    w_local.wait()


def attention(q, k, v, mk, mv, req, info, w):
    any_ = pl.BlockSpec(memory_space=pl.ANY)
    vm = pl.BlockSpec(memory_space=pltpu.VMEM)
    b16 = jnp.bfloat16
    hot = (8, BLOCK, HD)
    dma = pltpu.SemaphoreType.DMA
    return pl.pallas_call(
        attention_kernel,
        out_shape=(
            jax.ShapeDtypeStruct((2, ROWS, HD), b16),
            jax.ShapeDtypeStruct((2048, 512), b16),
        ),
        in_specs=[any_] * 5 + [vm, vm, any_],
        out_specs=(vm, any_),
        scratch_shapes=[
            pltpu.VMEM((2, ROWS, HD), b16),
            pltpu.VMEM((16, 2, ROWS, HD), b16),
            pltpu.VMEM((2, ROWS, HD), jnp.float32),
            pltpu.VMEM((2, ROWS, HD), jnp.float32),
            pltpu.VMEM((2, ROWS, HD), jnp.float32),
            pltpu.VMEM((64, BLOCK, 2 * HD), b16),
            pltpu.VMEM((64, BLOCK, 2 * HD), b16),
            pltpu.VMEM((16, 2, 2, 2, BLOCK, HD), b16),
            pltpu.VMEM((72, 2, BLOCK, HD), b16),
            pltpu.VMEM((TOPB * BLOCK, HD), b16),
            pltpu.VMEM((TOPB * BLOCK, HD), b16),
            pltpu.VMEM((2,) + hot, b16),
            pltpu.VMEM((2,) + hot, b16),
            pltpu.VMEM((2,) + hot, b16),
            pltpu.VMEM((2,) + hot, b16),
            pltpu.VMEM(hot, b16),
            pltpu.VMEM(hot, b16),
            pltpu.VMEM(hot, b16),
            pltpu.VMEM(hot, b16),
            pltpu.VMEM(hot, b16),
            pltpu.VMEM((16, 8, 128), jnp.int32),
            pltpu.VMEM((8, 128), jnp.int32),
            pltpu.SMEM((16, 8, 128), jnp.int32),
            pltpu.SMEM((2, 8, 128), jnp.int32),
            dma((10,)),
            dma((32,)),
            dma((28,)),
            dma((4,)),
            dma((1,)),
            dma((1,)),
            dma((16,)),
            dma((16,)),
            dma((32,)),
            dma((32,)),
            dma((5,)),
            dma((5,)),
            dma((8,)),
            dma((8,)),
        ],
        compiler_params=pltpu.CompilerParams(
            collective_id=0, has_side_effects=True, vmem_limit_bytes=56 << 20
        ),
        name="attention",
    )(q, k, v, mk, mv, req, info, w)


def gather_kernel(o_ref, a_ref, ybuf, send, recv, ysend, yrecv, loc_sem):
    s, hd, z, x, c, zh, y = where_am_i()
    up = zh * 4 + lax.rem(y + 1, 4)
    dn = zh * 4 + lax.rem(y + 3, 4)
    y1 = lax.rem(y + 3, 4)
    y2 = lax.rem(y + 1, 4)
    y3 = lax.rem(y + 2, 4)
    peers = [(1 - z, zh), (1 - z, 1 - zh), (z, 1 - zh)]
    bar = pltpu.get_barrier_semaphore()
    for zd, zhd in peers:
        pl.semaphore_signal(
            bar, inc=1, device_id=(seq_of(zd, x, c), zhd * 4 + y), device_id_type=MESH
        )
    pl.semaphore_signal(bar, inc=1, device_id=(s, up), device_id_type=MESH)
    pl.semaphore_signal(bar, inc=1, device_id=(s, dn), device_id_type=MESH)
    pl.semaphore_wait(bar, 5)

    def head_cols(zhs, ys, zs):
        return pl.ds(pl.multiple_of(((zhs * 4 + ys) * 2 + zs) * HD, HD), HD)

    def z_send(src, ys, p, n):
        zd, zhd = peers[p]
        return remote(
            src(zd), a_ref.at[:, head_cols(zh, ys, z)], send.at[n * 3 + p], recv.at[n * 3 + p],
            (seq_of(zd, x, c), zhd * 4 + y),
        )

    def z_wait(ys, p, n):
        zd, zhd = peers[p]
        remote(
            o_ref.at[0], a_ref.at[:, head_cols(zhd, ys, zd)], send.at[n * 3 + p],
            recv.at[n * 3 + p], (s, hd),
        ).wait_recv()

    own = pltpu.make_async_copy(o_ref.at[z], a_ref.at[:, head_cols(zh, y, z)], loc_sem.at[0])
    own.start()
    outs = [z_send(lambda zd: o_ref.at[zd], y, p, 0) for p in range(3)]

    @pl.when(c == 0)
    def _():
        for cp in outs:
            cp.start()
        own.wait()
        for p in range(3):
            z_wait(y, p, 0)

        def slab(zz, yy):
            return a_ref.at[:, pl.ds(pl.multiple_of((zz * 4 + yy) * 256, 256), 256)]

        def y_copy(n, zz, yy, dev):
            return remote(slab(zz, yy), slab(zz, yy), ysend.at[n], yrecv.at[yy * 2 + zz], (s, dev))

        sends = [y_copy(0, 0, y, up), y_copy(1, 1, y, dn), y_copy(2, 1, y, up), y_copy(3, 0, y, dn)]
        for cp in sends:
            cp.start()
        y_copy(0, 0, y1, up).wait_recv()
        f0 = y_copy(4, 0, y1, up)
        f0.start()
        y_copy(0, 1, y2, up).wait_recv()
        f1 = y_copy(5, 1, y2, dn)
        f1.start()
        for zz, yy in ((1, y1), (0, y2), (0, y3), (1, y3)):
            y_copy(0, zz, yy, up).wait_recv()
        for cp in outs + sends + [f0, f1]:
            cp.wait_send()

    @pl.when(c == 1)
    def _():
        def y_copy(n, h, yy, dev, first=False):
            src = o_ref.at[h] if first else ybuf.at[yy, h]
            return remote(src, ybuf.at[yy, h], ysend.at[n], yrecv.at[yy * 2 + h], (s, dev))

        sends = [
            y_copy(0, 0, y, up, True), y_copy(1, 1, y, dn, True),
            y_copy(2, 1, y, up, True), y_copy(3, 0, y, dn, True),
        ]
        for cp in sends:
            cp.start()
        for cp in outs:
            cp.start()
        y_copy(0, 0, y1, up).wait_recv()
        f0 = y_copy(4, 0, y1, up)
        f0.start()
        y_copy(0, 1, y2, up).wait_recv()
        f1 = y_copy(5, 1, y2, dn)
        f1.start()
        locs = []
        more = []

        def spread(yy, n):
            cps = [z_send(lambda zd: ybuf.at[yy, zd], yy, p, n) for p in range(3)]
            for cp in cps:
                cp.start()
            lc = pltpu.make_async_copy(
                ybuf.at[yy, z], a_ref.at[:, head_cols(zh, yy, z)], loc_sem.at[n]
            )
            lc.start()
            more.extend(cps)
            locs.append(lc)

        y_copy(0, 1, y1, up).wait_recv()
        spread(y1, 1)
        y_copy(0, 0, y2, up).wait_recv()
        spread(y2, 2)
        y_copy(0, 0, y3, up).wait_recv()
        y_copy(0, 1, y3, up).wait_recv()
        spread(y3, 3)
        own.wait()
        for lc in locs:
            lc.wait()
        for n, yy in enumerate((y, y1, y2, y3)):
            for p in range(3):
                z_wait(yy, p, n)
        for cp in outs + sends + more + [f0, f1]:
            cp.wait_send()


def gather(o):
    dma = pltpu.SemaphoreType.DMA
    vm = pl.BlockSpec(memory_space=pltpu.VMEM)
    return pl.pallas_call(
        gather_kernel,
        out_shape=jax.ShapeDtypeStruct((ROWS, 2048), jnp.bfloat16),
        in_specs=[vm],
        out_specs=vm,
        scratch_shapes=[
            pltpu.VMEM((4, 2, ROWS, HD), jnp.bfloat16),
            dma((12,)), dma((12,)), dma((6,)), dma((8,)), dma((4,)),
        ],
        compiler_params=pltpu.CompilerParams(
            collective_id=1, has_side_effects=True, vmem_limit_bytes=32 << 20
        ),
        name="gather_heads",
    )(o)


def tables(block_index):
    z = lax.axis_index("seq") // 8
    w = block_index.reshape(-1)
    holder = w // 64
    local = w - holder * 64
    owners = jnp.arange(16, dtype=jnp.int32)
    n = jnp.arange(32, dtype=jnp.int32)
    same = holder[:, None] == holder[None, :]
    count = jnp.sum(same.astype(jnp.int32), axis=1)
    place = jnp.sum((same & (n[None, :] < n[:, None])).astype(jnp.int32), axis=1)
    is_hot = count == TOPB
    rank = jnp.sum((same & (local[None, :] < local[:, None])).astype(jnp.int32), axis=1)
    lanes = jnp.arange(128, dtype=jnp.int32)
    hit = (holder[:, None, None] == owners[None, :, None]) & (
        place[:, None, None] == lanes[None, None, :]
    ) & (lanes < 2)[None, None, :]
    req = jnp.sum(jnp.where(hit, local[:, None, None], 0), axis=0)
    code = jnp.where(is_hot, 64 + rank, (z * 16 + holder) * 2 + place)
    at_code = n[:, None] == lanes[None, :]
    at_hot = is_hot[:, None] & ((rank + 32)[:, None] == lanes[None, :])
    at_owner = (is_hot & (rank == 0))[:, None] & (lanes == 40)[None, :]
    info = jnp.sum(
        jnp.where(at_code, code[:, None], 0)
        + jnp.where(at_hot, local[:, None], 0)
        + jnp.where(at_owner, holder[:, None], 0),
        axis=0,
    )
    return (
        jnp.broadcast_to(req[:, None, :], (16, 8, 128)),
        jnp.broadcast_to(info[None, :], (8, 128)),
    )


def shards(q, k, v, mk, mv, block_index, w):
    req, info = tables(block_index)
    o, wc = attention(
        q, k, v, mk.reshape(-1, BLOCK, 2 * HD), mv.reshape(-1, BLOCK, 2 * HD), req, info, w
    )
    a = gather(o)
    return jnp.dot(a, wc, preferred_element_type=jnp.float32).astype(jnp.bfloat16)


def solution(mesh):
    return jax.shard_map(
        shards,
        mesh=mesh,
        in_specs=(
            P("seq", "head"), P("seq", "head"), P("seq", "head"), P("seq", "head"),
            P("seq", "head"), P("seq", None), P("head", None),
        ),
        out_specs=P("seq", "head"),
        check_vma=False,
    )
```

```python
import functools
import math

import jax
import jax.numpy as jnp
from jax import lax
from jax.experimental import pallas as pl
from jax.experimental.pallas import tpu as pltpu
from jax.sharding import PartitionSpec as P

MESH = pl.DeviceIdType.MESH
HD = 128
GROUP = 256
BLOCK = 64
TOPB = 8
ROWS = 1024
CHUNK = 256
SCALE = math.log2(math.e) / math.sqrt(HD)
LOW = -1e30
STEPS = 24
GATHER_AT = 1
MEM_NEAR = 9
MEM_FAR = 12


def where_am_i():
    s = lax.axis_index("seq")
    hd = lax.axis_index("head")
    return s, hd, s // 8, (s // 2) % 4, s % 2, hd // 4, hd % 4


def seq_of(z, x, c):
    return z * 8 + x * 2 + c


def dot_nt(a, b):
    return lax.dot_general(a, b, (((1,), (1,)), ((), ())), preferred_element_type=jnp.float32)


def pick(t, table, default):
    out = default
    for k, v in table.items():
        out = jnp.where(t == k, v, out)
    return out


def remote(src, dst, ss, rs, dev):
    return pltpu.make_async_remote_copy(
        src_ref=src, dst_ref=dst, send_sem=ss, recv_sem=rs, device_id=dev, device_id_type=MESH
    )


DXS = (0, 0, 3, 1, 3, 1, 2, 2)
SIBS = (0, 1, 0, 0, 1, 1, 0, 1)
SERVICE_A = {1: 1, 2: 2, 3: 8, 4: 4, 5: 5, 6: 6, 7: 7, 10: 9, 12: 10, 16: 12, 18: 13, 20: 14, 22: 15}
SERVICE_B = {2: 3, 12: 11}


def attention_kernel(
    q_hbm, k_hbm, v_hbm, mk_hbm, mv_hbm, req_ref, info_ref, w_hbm,
    o_ref, wc_hbm,
    q, kv, m_s, l_s, acc, mk, mv, stage, mem, hot, kc, vc,
    reqin, infoin, reqs, infos,
    loc_sem, kv_recv, ring_send, swap_send, q_recv, info_recv,
    req_send, req_recv, mem_send, mem_recv, hot_send, hot_recv, w_send, w_recv,
):
    s, hd, z, x, c, zh, y = where_am_i()
    zp = seq_of(1 - z, x, c)
    sib = seq_of(z, x, 1 - c)
    xr = seq_of(z, lax.rem(x + 1, 4), c)
    xl = seq_of(z, lax.rem(x + 3, 4), c)

    mine = pl.ds(pl.multiple_of(z * HD, HD), HD)
    theirs = pl.ds(pl.multiple_of((1 - z) * HD, HD), HD)
    loc = [
        pltpu.make_async_copy(k_hbm.at[:, mine], kv.at[s, 0], loc_sem.at[0]),
        pltpu.make_async_copy(v_hbm.at[:, mine], kv.at[s, 1], loc_sem.at[1]),
        pltpu.make_async_copy(q_hbm.at[:, mine], q.at[z], loc_sem.at[2]),
        pltpu.make_async_copy(mk_hbm, mk, loc_sem.at[3]),
        pltpu.make_async_copy(mv_hbm, mv, loc_sem.at[4]),
        pltpu.make_async_copy(info_ref, infos.at[z], loc_sem.at[5]),
        pltpu.make_async_copy(req_ref.at[s], reqin.at[s], loc_sem.at[6]),
    ]
    for cp in loc:
        cp.start()

    bar = pltpu.get_barrier_semaphore()

    def w_target(i):
        same = (i // 4) == zh
        zd = jnp.where(same, z, 1 - z)
        return (seq_of(zd, x, c), i)

    def greet(i, _):
        @pl.when(i != s)
        def _():
            pl.semaphore_signal(bar, inc=1, device_id=(i, hd), device_id_type=MESH)
        return 0

    lax.fori_loop(0, 16, greet, 0)

    def greet_w(i, _):
        @pl.when(i != hd)
        def _():
            pl.semaphore_signal(bar, inc=1, device_id=w_target(i), device_id_type=MESH)
        return 0

    lax.fori_loop(0, 8, greet_w, 0)
    pl.semaphore_wait(bar, 22)

    swaps = [
        remote(k_hbm.at[:, theirs], kv.at[s, 0], swap_send.at[0], kv_recv.at[s * 2], (zp, hd)),
        remote(v_hbm.at[:, theirs], kv.at[s, 1], swap_send.at[1], kv_recv.at[s * 2 + 1], (zp, hd)),
        remote(info_ref, infoin, swap_send.at[2], info_recv.at[0], (zp, hd)),
        remote(q_hbm.at[:, theirs], q.at[z], swap_send.at[3], q_recv.at[0], (zp, hd)),
    ]
    swaps[2].start()

    def req_copy(i):
        return remote(req_ref.at[i], reqin.at[s], req_send.at[i], req_recv.at[s], (i, hd))

    def send_req(i, _):
        @pl.when(i != s)
        def _():
            req_copy(i).start()
        return 0

    lax.fori_loop(0, 16, send_req, 0)
    swaps[0].start()
    swaps[1].start()

    def ring_copy(half, n, g, k, dev):
        return remote(
            kv.at[g, k], kv.at[g, k], ring_send.at[half * 14 + n], kv_recv.at[g * 2 + k], (dev, hd)
        )

    def sends_of(kind, half, g, k):
        if kind == 0:
            n = 3 * k
            return [
                ring_copy(half, n, g, k, xr), ring_copy(half, n + 1, g, k, xl),
                ring_copy(half, n + 2, g, k, sib),
            ]
        if kind == 2:
            on = [ring_copy(half, 6, g, 0, xr)] if k == 0 else []
            return on + [ring_copy(half, 7 + k, g, k, sib)]
        if kind == 3:
            on = [ring_copy(half, 9, g, 1, xl)] if k == 1 else []
            return on + [ring_copy(half, 10 + k, g, k, sib)]
        return [ring_copy(half, 12 + k, g, k, sib)]

    def block_of(half, i):
        dx = pick(i, dict(enumerate(DXS)), 0)
        sb = pick(i, dict(enumerate(SIBS)), 0)
        return seq_of(half, lax.rem(x + dx, 4), jnp.where(sb == 1, 1 - c, c))

    for k in range(2):
        loc[k].wait()
        for cp in sends_of(0, z, s, k):
            cp.start()
    swaps[3].start()

    def w_copy(i):
        cols = pl.ds(pl.multiple_of(i * 512, 512), 512)
        rows = pl.ds(pl.multiple_of(hd * 256, 256), 256)
        return remote(
            w_hbm.at[:, cols], wc_hbm.at[rows, :], w_send.at[i], w_recv.at[hd], w_target(i)
        )

    def send_w(i, _):
        @pl.when(i != hd)
        def _():
            w_copy(i).start()
        return 0

    lax.fori_loop(0, 8, send_w, 0)
    w_local = pltpu.make_async_copy(
        w_hbm.at[:, pl.ds(pl.multiple_of(hd * 512, 512), 512)],
        wc_hbm.at[pl.ds(pl.multiple_of(hd * 256, 256), 256), :],
        loc_sem.at[7],
    )
    w_local.start()

    m_s[...] = jnp.full_like(m_s, LOW)
    l_s[...] = jnp.zeros_like(l_s)
    acc[...] = jnp.zeros_like(acc)

    def wait_part(g, k):
        remote(kv.at[g, k], kv.at[g, k], ring_send.at[0], kv_recv.at[g * 2 + k], (sib, hd)).wait_recv()

    def service(code):
        @pl.when(code >= 0)
        def _():
            half = jnp.where(code >= 8, 1 - z, z)
            i = lax.rem(code, 8)
            g = block_of(half, i)
            for k in range(2):
                wait_part(g, k)
                for kind in (0, 2, 3, 6):
                    @pl.when(i == kind)
                    def _(kind=kind):
                        for cp in sends_of(kind, half, g, k):
                            cp.start()

    def pipelined(n, scores, finish):
        state = scores(0)
        for j in range(n):
            later = scores(j + 1) if j + 1 < n else None
            finish(j, state)
            state = later

    def absorb(qh, rows, sc, val):
        mo = m_s[qh, rows, :]
        mn = jnp.maximum(mo, jnp.max(sc, axis=-1, keepdims=True))
        m_s[qh, rows, :] = mn
        return sc, mo, mn, val

    def settle(qh, rows, state):
        sc, mo, mn, val = state
        p = jnp.exp2((sc - mn[:, :1]) * SCALE)
        sh = jnp.exp2((mo - mn) * SCALE)
        ls = p[:, 0:128]
        for u in range(1, p.shape[1] // 128):
            ls = ls + p[:, u * 128:(u + 1) * 128]
        l_s[qh, rows, :] = l_s[qh, rows, :] * sh + ls
        acc[qh, rows, :] = acc[qh, rows, :] * sh + jnp.dot(
            p.astype(jnp.bfloat16), val(), preferred_element_type=jnp.float32
        )

    def attend(qh, g):
        gq = seq_of(qh, x, c)

        @pl.when(g < gq)
        def _():
            def scores(j):
                rows = pl.ds(j * CHUNK, CHUNK)
                return absorb(
                    qh, rows, dot_nt(q[qh, rows, :], kv[g, 0, :, :]), lambda: kv[g, 1, :, :]
                )

            pipelined(ROWS // CHUNK, scores, lambda j, st: settle(qh, pl.ds(j * CHUNK, CHUNK), st))

        @pl.when(g == gq)
        def _():
            def scores(j):
                rows = pl.ds(j * CHUNK, CHUNK)
                n = (j + 1) * CHUNK
                sc = dot_nt(q[qh, rows, :], kv[g, 0, 0:n, :])
                last = sc[:, n - CHUNK:]
                ok = lax.broadcasted_iota(jnp.int32, (CHUNK, CHUNK), 1) <= lax.broadcasted_iota(
                    jnp.int32, (CHUNK, CHUNK), 0
                )
                last = jnp.where(ok, last, LOW)
                if j:
                    last = jnp.concatenate([sc[:, : n - CHUNK], last], axis=1)
                return absorb(qh, rows, last, lambda: kv[g, 1, 0:n, :])

            pipelined(ROWS // CHUNK, scores, lambda j, st: settle(qh, pl.ds(j * CHUNK, CHUNK), st))

    def mem_copy(r, e):
        dst = seq_of(e, (r // 2) % 4, lax.rem(r, 2))
        at = (r // 8) * 16 + s
        return dst, at

    def pair(at):
        return mem.at[pl.ds(at * 2, 2)]

    def mem_remote(r, e):
        dst, at = mem_copy(r, e)
        return remote(
            stage.at[r, e], pair(at), mem_send.at[r * 2 + e], mem_recv.at[at], (dst, hd)
        )

    def hot_copies(n):
        at = pl.ds(4 * n + 2 * c, 2)
        return remote(hot.at[at], hot.at[at], hot_send.at[n], hot_recv.at[n], (sib, hd))

    def step(t, _):
        @pl.when(t == 8)
        def _():
            remote(q.at[0], q.at[1 - z], swap_send.at[3], q_recv.at[0], (zp, hd)).wait_recv()

        service(pick(t, SERVICE_A, -1))
        service(pick(t, SERVICE_B, -1))

        @pl.when(t == GATHER_AT)
        def _():
            def wait_req(i, _):
                @pl.when(i != s)
                def _():
                    remote(
                        req_ref.at[i], reqin.at[i], req_send.at[i], req_recv.at[i], (sib, hd)
                    ).wait_recv()
                return 0

            lax.fori_loop(0, 16, wait_req, 0)
            swaps[2].wait_recv()
            for cp in loc[3:]:
                cp.wait()
            a = pltpu.make_async_copy(reqin, reqs, loc_sem.at[8])
            b = pltpu.make_async_copy(infoin, infos.at[1 - z], loc_sem.at[9])
            a.start()
            b.start()
            a.wait()
            b.wait()

            def gather(r, _):
                for b2 in range(2):
                    b = reqs[r, 0, b2]
                    kr = mk[b]
                    vr = mv[b]
                    for e in range(2):
                        cols = slice(e * HD, (e + 1) * HD)
                        stage[r, e, b2, 0] = kr[:, cols]
                        stage[r, e, b2, 1] = vr[:, cols]
                return 0

            lax.fori_loop(0, 16, gather, 0)

        @pl.when((t == MEM_NEAR) | (t == MEM_FAR))
        def _():
            def send(i, _):
                r = lax.rem(i + s + 1, 16)
                e = jnp.where(t == MEM_NEAR, z, 1 - z)
                dst, at = mem_copy(r, e)

                @pl.when(dst == s)
                def _():
                    pltpu.make_async_copy(stage.at[r, e], pair(at), mem_recv.at[at]).start()

                @pl.when(dst != s)
                def _():
                    mem_remote(r, e).start()
                return 0

            lax.fori_loop(0, 16, send, 0)

        native = t < 8
        u = t - 8
        qh = jnp.where(native, z, jnp.where(z == 0, 1, lax.rem(t, 2)))
        half = jnp.where(native, z, jnp.where((z == 0) & (u >= 8), 1, 0))
        i = jnp.where(native, t, jnp.where(z == 0, lax.rem(t, 8), u // 2))
        attend(qh, block_of(half, i))
        return 0

    loc[2].wait()
    lax.fori_loop(0, STEPS, step, 0)

    def wait_mem(i, _):
        own = lax.rem(i, 16) == s

        @pl.when(jnp.logical_not(own))
        def _():
            remote(
                stage.at[0, 0], pair(i), mem_send.at[0], mem_recv.at[i], (sib, hd)
            ).wait_recv()

        @pl.when(own)
        def _():
            pltpu.make_async_copy(stage.at[0, 0], pair(i), mem_recv.at[i]).wait()
        return 0

    lax.fori_loop(0, 32, wait_mem, 0)
    ho = infos[z, 0, 40]
    for n in range(2):
        for b2 in range(2):
            hot[4 * n + 2 * c + b2] = mem[(n * 16 + ho) * 2 + b2]
        hot_copies(n).start()
    for n in range(2):
        at = pl.ds(4 * n + 2 * (1 - c), 2)
        remote(hot.at[at], hot.at[at], hot_send.at[n], hot_recv.at[n], (sib, hd)).wait_recv()
    for j in range(8):
        mem[64 + j] = hot[j]

    def mem_group(i, _):
        qh = i // 4
        j = lax.rem(i, 4)
        for e in range(TOPB):
            code = infos[qh, 0, j * TOPB + e]
            kc[e * BLOCK:(e + 1) * BLOCK, :] = mem[code, 0]
            vc[e * BLOCK:(e + 1) * BLOCK, :] = mem[code, 1]
        rows = pl.ds(pl.multiple_of(j * GROUP, GROUP), GROUP)
        st = absorb(qh, rows, dot_nt(q[qh, rows, :], kc[...]), lambda: vc[...])
        settle(qh, rows, st)
        o_ref[qh, rows, :] = (
            acc[qh, rows, :] / jnp.sum(l_s[qh, rows, :], axis=-1, keepdims=True)
        ).astype(jnp.bfloat16)
        return 0

    lax.fori_loop(0, 8, mem_group, 0)

    for cp in swaps:
        cp.wait_send()
    for half in (0, 1):
        for kind in (0, 2, 3, 6):
            for k in range(2):
                for cp in sends_of(kind, half, s, k):
                    cp.wait_send()
    for n in range(2):
        hot_copies(n).wait_send()

    def drain_req(i, _):
        @pl.when(i != s)
        def _():
            req_copy(i).wait_send()
        return 0

    lax.fori_loop(0, 16, drain_req, 0)

    def drain_mem(i, _):
        dst, _at = mem_copy(i // 2, lax.rem(i, 2))

        @pl.when(dst != s)
        def _():
            mem_remote(i // 2, lax.rem(i, 2)).wait_send()
        return 0

    lax.fori_loop(0, 32, drain_mem, 0)

    def drain_w(i, _):
        @pl.when(i != hd)
        def _():
            w_copy(i).wait_send()
            rows = pl.ds(pl.multiple_of(i * 256, 256), 256)
            remote(
                w_hbm.at[:, pl.ds(0, 512)], wc_hbm.at[rows, :], w_send.at[i], w_recv.at[i], (sib, hd)
            ).wait_recv()
        return 0

    lax.fori_loop(0, 8, drain_w, 0)
    w_local.wait()


def attention(q, k, v, mk, mv, req, info, w):
    any_ = pl.BlockSpec(memory_space=pl.ANY)
    vm = pl.BlockSpec(memory_space=pltpu.VMEM)
    b16 = jnp.bfloat16
    dma = pltpu.SemaphoreType.DMA
    return pl.pallas_call(
        attention_kernel,
        out_shape=(
            jax.ShapeDtypeStruct((2, ROWS, HD), b16),
            jax.ShapeDtypeStruct((2048, 512), b16),
        ),
        in_specs=[any_] * 5 + [vm, vm, any_],
        out_specs=(vm, any_),
        scratch_shapes=[
            pltpu.VMEM((2, ROWS, HD), b16),
            pltpu.VMEM((16, 2, ROWS, HD), b16),
            pltpu.VMEM((2, ROWS, HD), jnp.float32),
            pltpu.VMEM((2, ROWS, HD), jnp.float32),
            pltpu.VMEM((2, ROWS, HD), jnp.float32),
            pltpu.VMEM((64, BLOCK, 2 * HD), b16),
            pltpu.VMEM((64, BLOCK, 2 * HD), b16),
            pltpu.VMEM((16, 2, 2, 2, BLOCK, HD), b16),
            pltpu.VMEM((72, 2, BLOCK, HD), b16),
            pltpu.VMEM((8, 2, BLOCK, HD), b16),
            pltpu.VMEM((TOPB * BLOCK, HD), b16),
            pltpu.VMEM((TOPB * BLOCK, HD), b16),
            pltpu.VMEM((16, 8, 128), jnp.int32),
            pltpu.VMEM((8, 128), jnp.int32),
            pltpu.SMEM((16, 8, 128), jnp.int32),
            pltpu.SMEM((2, 8, 128), jnp.int32),
            dma((10,)),
            dma((32,)),
            dma((28,)),
            dma((4,)),
            dma((1,)),
            dma((1,)),
            dma((16,)),
            dma((16,)),
            dma((32,)),
            dma((32,)),
            dma((2,)),
            dma((2,)),
            dma((8,)),
            dma((8,)),
        ],
        compiler_params=pltpu.CompilerParams(
            collective_id=0, has_side_effects=True, vmem_limit_bytes=56 << 20
        ),
        name="attention",
    )(q, k, v, mk, mv, req, info, w)


def gather_kernel(o_ref, a_ref, ybuf, send, recv, ysend, yrecv, loc_sem):
    s, hd, z, x, c, zh, y = where_am_i()
    up = zh * 4 + lax.rem(y + 1, 4)
    dn = zh * 4 + lax.rem(y + 3, 4)
    y1 = lax.rem(y + 3, 4)
    y2 = lax.rem(y + 1, 4)
    y3 = lax.rem(y + 2, 4)
    peers = [(1 - z, zh), (1 - z, 1 - zh), (z, 1 - zh)]
    bar = pltpu.get_barrier_semaphore()
    for zd, zhd in peers:
        pl.semaphore_signal(
            bar, inc=1, device_id=(seq_of(zd, x, c), zhd * 4 + y), device_id_type=MESH
        )
    pl.semaphore_signal(bar, inc=1, device_id=(s, up), device_id_type=MESH)
    pl.semaphore_signal(bar, inc=1, device_id=(s, dn), device_id_type=MESH)
    pl.semaphore_wait(bar, 5)

    def head_cols(zhs, ys, zs):
        return pl.ds(pl.multiple_of(((zhs * 4 + ys) * 2 + zs) * HD, HD), HD)

    def z_send(src, ys, p, n):
        zd, zhd = peers[p]
        return remote(
            src(zd), a_ref.at[:, head_cols(zh, ys, z)], send.at[n * 3 + p], recv.at[n * 3 + p],
            (seq_of(zd, x, c), zhd * 4 + y),
        )

    def z_wait(ys, p, n):
        zd, zhd = peers[p]
        remote(
            o_ref.at[0], a_ref.at[:, head_cols(zhd, ys, zd)], send.at[n * 3 + p],
            recv.at[n * 3 + p], (s, hd),
        ).wait_recv()

    own = pltpu.make_async_copy(o_ref.at[z], a_ref.at[:, head_cols(zh, y, z)], loc_sem.at[0])
    own.start()
    outs = [z_send(lambda zd: o_ref.at[zd], y, p, 0) for p in range(3)]

    @pl.when(c == 0)
    def _():
        for cp in outs:
            cp.start()
        own.wait()
        for p in range(3):
            z_wait(y, p, 0)

        def slab(zz, yy):
            return a_ref.at[:, pl.ds(pl.multiple_of((zz * 4 + yy) * 256, 256), 256)]

        def y_copy(n, zz, yy, dev):
            return remote(slab(zz, yy), slab(zz, yy), ysend.at[n], yrecv.at[yy * 2 + zz], (s, dev))

        sends = [y_copy(0, 0, y, up), y_copy(1, 1, y, dn), y_copy(2, 1, y, up), y_copy(3, 0, y, dn)]
        for cp in sends:
            cp.start()
        y_copy(0, 0, y1, up).wait_recv()
        f0 = y_copy(4, 0, y1, up)
        f0.start()
        y_copy(0, 1, y2, up).wait_recv()
        f1 = y_copy(5, 1, y2, dn)
        f1.start()
        for zz, yy in ((1, y1), (0, y2), (0, y3), (1, y3)):
            y_copy(0, zz, yy, up).wait_recv()
        for cp in outs + sends + [f0, f1]:
            cp.wait_send()

    @pl.when(c == 1)
    def _():
        def y_copy(n, h, yy, dev, first=False):
            src = o_ref.at[h] if first else ybuf.at[yy, h]
            return remote(src, ybuf.at[yy, h], ysend.at[n], yrecv.at[yy * 2 + h], (s, dev))

        sends = [
            y_copy(0, 0, y, up, True), y_copy(1, 1, y, dn, True),
            y_copy(2, 1, y, up, True), y_copy(3, 0, y, dn, True),
        ]
        for cp in sends:
            cp.start()
        for cp in outs:
            cp.start()
        y_copy(0, 0, y1, up).wait_recv()
        f0 = y_copy(4, 0, y1, up)
        f0.start()
        y_copy(0, 1, y2, up).wait_recv()
        f1 = y_copy(5, 1, y2, dn)
        f1.start()
        locs = []
        more = []

        def spread(yy, n):
            cps = [z_send(lambda zd: ybuf.at[yy, zd], yy, p, n) for p in range(3)]
            for cp in cps:
                cp.start()
            lc = pltpu.make_async_copy(
                ybuf.at[yy, z], a_ref.at[:, head_cols(zh, yy, z)], loc_sem.at[n]
            )
            lc.start()
            more.extend(cps)
            locs.append(lc)

        y_copy(0, 1, y1, up).wait_recv()
        spread(y1, 1)
        y_copy(0, 0, y2, up).wait_recv()
        spread(y2, 2)
        y_copy(0, 0, y3, up).wait_recv()
        y_copy(0, 1, y3, up).wait_recv()
        spread(y3, 3)
        own.wait()
        for lc in locs:
            lc.wait()
        for n, yy in enumerate((y, y1, y2, y3)):
            for p in range(3):
                z_wait(yy, p, n)
        for cp in outs + sends + more + [f0, f1]:
            cp.wait_send()


def gather(o):
    dma = pltpu.SemaphoreType.DMA
    vm = pl.BlockSpec(memory_space=pltpu.VMEM)
    return pl.pallas_call(
        gather_kernel,
        out_shape=jax.ShapeDtypeStruct((ROWS, 2048), jnp.bfloat16),
        in_specs=[vm],
        out_specs=vm,
        scratch_shapes=[
            pltpu.VMEM((4, 2, ROWS, HD), jnp.bfloat16),
            dma((12,)), dma((12,)), dma((6,)), dma((8,)), dma((4,)),
        ],
        compiler_params=pltpu.CompilerParams(
            collective_id=1, has_side_effects=True, vmem_limit_bytes=32 << 20
        ),
        name="gather_heads",
    )(o)


def tables(block_index):
    z = lax.axis_index("seq") // 8
    w = block_index.reshape(-1)
    holder = w // 64
    local = w - holder * 64
    owners = jnp.arange(16, dtype=jnp.int32)
    n = jnp.arange(32, dtype=jnp.int32)
    same = holder[:, None] == holder[None, :]
    count = jnp.sum(same.astype(jnp.int32), axis=1)
    place = jnp.sum((same & (n[None, :] < n[:, None])).astype(jnp.int32), axis=1)
    is_hot = count == TOPB
    rank = jnp.sum((same & (local[None, :] < local[:, None])).astype(jnp.int32), axis=1)
    lanes = jnp.arange(128, dtype=jnp.int32)
    mine = z * 2 + lax.axis_index("seq") % 2
    slot = jnp.where(is_hot, rank - 2 * mine, place)
    hit = (holder[:, None, None] == owners[None, :, None]) & (
        slot[:, None, None] == lanes[None, None, :]
    ) & (lanes < 2)[None, None, :]
    req = jnp.sum(jnp.where(hit, local[:, None, None], 0), axis=0)
    code = jnp.where(is_hot, 64 + rank, (z * 16 + holder) * 2 + place)
    at_code = n[:, None] == lanes[None, :]
    at_hot = is_hot[:, None] & ((rank + 32)[:, None] == lanes[None, :])
    at_owner = (is_hot & (rank == 0))[:, None] & (lanes == 40)[None, :]
    info = jnp.sum(
        jnp.where(at_code, code[:, None], 0)
        + jnp.where(at_hot, local[:, None], 0)
        + jnp.where(at_owner, holder[:, None], 0),
        axis=0,
    )
    return (
        jnp.broadcast_to(req[:, None, :], (16, 8, 128)),
        jnp.broadcast_to(info[None, :], (8, 128)),
    )


def shards(q, k, v, mk, mv, block_index, w):
    req, info = tables(block_index)
    o, wc = attention(
        q, k, v, mk.reshape(-1, BLOCK, 2 * HD), mv.reshape(-1, BLOCK, 2 * HD), req, info, w
    )
    a = gather(o)
    return jnp.dot(a, wc, preferred_element_type=jnp.float32).astype(jnp.bfloat16)


def solution(mesh):
    return jax.shard_map(
        shards,
        mesh=mesh,
        in_specs=(
            P("seq", "head"), P("seq", "head"), P("seq", "head"), P("seq", "head"),
            P("seq", "head"), P("seq", None), P("head", None),
        ),
        out_specs=P("seq", "head"),
        check_vma=False,
    )
```

```python
import functools
import math

import jax
import jax.numpy as jnp
from jax import lax
from jax.experimental import pallas as pl
from jax.experimental.pallas import tpu as pltpu
from jax.sharding import PartitionSpec as P

MESH = pl.DeviceIdType.MESH
HD = 128
GROUP = 256
BLOCK = 64
TOPB = 8
ROWS = 1024
CHUNK = 256
SCALE = math.log2(math.e) / math.sqrt(HD)
LOW = -1e30
STEPS = 24
GATHER_AT = 1
MEM_NEAR = 9
MEM_FAR = 12


def where_am_i():
    s = lax.axis_index("seq")
    hd = lax.axis_index("head")
    return s, hd, s // 8, (s // 2) % 4, s % 2, hd // 4, hd % 4


def seq_of(z, x, c):
    return z * 8 + x * 2 + c


def dot_nt(a, b):
    return lax.dot_general(a, b, (((1,), (1,)), ((), ())), preferred_element_type=jnp.float32)


def pick(t, table, default):
    out = default
    for k, v in table.items():
        out = jnp.where(t == k, v, out)
    return out


def remote(src, dst, ss, rs, dev):
    return pltpu.make_async_remote_copy(
        src_ref=src, dst_ref=dst, send_sem=ss, recv_sem=rs, device_id=dev, device_id_type=MESH
    )


DXS = (0, 0, 3, 1, 3, 1, 2, 2)
SIBS = (0, 1, 0, 0, 1, 1, 0, 1)
SERVICE_A = {1: 1, 2: 2, 3: 8, 4: 4, 5: 5, 6: 6, 7: 7, 10: 9, 12: 10, 16: 12, 18: 13, 20: 14, 22: 15}
SERVICE_B = {2: 3, 12: 11}


def attention_kernel(
    q_hbm, k_hbm, v_hbm, mk_hbm, mv_hbm, req_ref, info_ref, w_hbm,
    out_ref,
    q, kv, m_s, l_s, acc, mk, mv, stage, mem, hot, kc, vc, o, ybuf, a_ref, wc, total,
    reqin, infoin, reqs, infos,
    loc_sem, kv_recv, ring_send, swap_send, q_recv, info_recv,
    req_send, req_recv, mem_send, mem_recv, hot_send, hot_recv, w_send, w_recv,
    zs, zr, ys, yr, as_,
):
    s, hd, z, x, c, zh, y = where_am_i()
    up = zh * 4 + lax.rem(y + 1, 4)
    dn = zh * 4 + lax.rem(y + 3, 4)
    yy1 = lax.rem(y + 3, 4)
    yy2 = lax.rem(y + 1, 4)
    yy3 = lax.rem(y + 2, 4)
    zp = seq_of(1 - z, x, c)
    sib = seq_of(z, x, 1 - c)
    xr = seq_of(z, lax.rem(x + 1, 4), c)
    xl = seq_of(z, lax.rem(x + 3, 4), c)

    mine = pl.ds(pl.multiple_of(z * HD, HD), HD)
    theirs = pl.ds(pl.multiple_of((1 - z) * HD, HD), HD)
    loc = [
        pltpu.make_async_copy(k_hbm.at[:, mine], kv.at[s, 0], loc_sem.at[0]),
        pltpu.make_async_copy(v_hbm.at[:, mine], kv.at[s, 1], loc_sem.at[1]),
        pltpu.make_async_copy(q_hbm.at[:, mine], q.at[z], loc_sem.at[2]),
        pltpu.make_async_copy(mk_hbm, mk, loc_sem.at[3]),
        pltpu.make_async_copy(mv_hbm, mv, loc_sem.at[4]),
        pltpu.make_async_copy(info_ref, infos.at[z], loc_sem.at[5]),
        pltpu.make_async_copy(req_ref.at[s], reqin.at[s], loc_sem.at[6]),
    ]
    for cp in loc:
        cp.start()

    bar = pltpu.get_barrier_semaphore()

    def w_target(i):
        same = (i // 4) == zh
        zd = jnp.where(same, z, 1 - z)
        return (seq_of(zd, x, c), i)

    def greet(i, _):
        @pl.when(i != s)
        def _():
            pl.semaphore_signal(bar, inc=1, device_id=(i, hd), device_id_type=MESH)
        return 0

    lax.fori_loop(0, 16, greet, 0)

    def greet_w(i, _):
        @pl.when(i != hd)
        def _():
            pl.semaphore_signal(bar, inc=1, device_id=w_target(i), device_id_type=MESH)
        return 0

    lax.fori_loop(0, 8, greet_w, 0)
    pl.semaphore_signal(bar, inc=1, device_id=(s, (1 - zh) * 4 + y), device_id_type=MESH)
    pl.semaphore_wait(bar, 23)

    swaps = [
        remote(k_hbm.at[:, theirs], kv.at[s, 0], swap_send.at[0], kv_recv.at[s * 2], (zp, hd)),
        remote(v_hbm.at[:, theirs], kv.at[s, 1], swap_send.at[1], kv_recv.at[s * 2 + 1], (zp, hd)),
        remote(info_ref, infoin, swap_send.at[2], info_recv.at[0], (zp, hd)),
        remote(q_hbm.at[:, theirs], q.at[z], swap_send.at[3], q_recv.at[0], (zp, hd)),
    ]
    swaps[2].start()

    def req_copy(i):
        return remote(req_ref.at[i], reqin.at[s], req_send.at[i], req_recv.at[s], (i, hd))

    def send_req(i, _):
        @pl.when(i != s)
        def _():
            req_copy(i).start()
        return 0

    lax.fori_loop(0, 16, send_req, 0)
    swaps[0].start()
    swaps[1].start()

    def ring_copy(half, n, g, k, dev):
        return remote(
            kv.at[g, k], kv.at[g, k], ring_send.at[half * 14 + n], kv_recv.at[g * 2 + k], (dev, hd)
        )

    def sends_of(kind, half, g, k):
        if kind == 0:
            n = 3 * k
            return [
                ring_copy(half, n, g, k, xr), ring_copy(half, n + 1, g, k, xl),
                ring_copy(half, n + 2, g, k, sib),
            ]
        if kind == 2:
            on = [ring_copy(half, 6, g, 0, xr)] if k == 0 else []
            return on + [ring_copy(half, 7 + k, g, k, sib)]
        if kind == 3:
            on = [ring_copy(half, 9, g, 1, xl)] if k == 1 else []
            return on + [ring_copy(half, 10 + k, g, k, sib)]
        return [ring_copy(half, 12 + k, g, k, sib)]

    def block_of(half, i):
        dx = pick(i, dict(enumerate(DXS)), 0)
        sb = pick(i, dict(enumerate(SIBS)), 0)
        return seq_of(half, lax.rem(x + dx, 4), jnp.where(sb == 1, 1 - c, c))

    for k in range(2):
        loc[k].wait()
        for cp in sends_of(0, z, s, k):
            cp.start()
    swaps[3].start()

    def w_copy(i):
        cols = pl.ds(pl.multiple_of(i * 512, 512), 512)
        rows = pl.ds(pl.multiple_of(hd * 256, 256), 256)
        return remote(
            w_hbm.at[:, cols], wc.at[rows, :], w_send.at[i], w_recv.at[hd], w_target(i)
        )

    def send_w(i, _):
        @pl.when(i != hd)
        def _():
            w_copy(i).start()
        return 0

    lax.fori_loop(0, 8, send_w, 0)
    w_local = pltpu.make_async_copy(
        w_hbm.at[:, pl.ds(pl.multiple_of(hd * 512, 512), 512)],
        wc.at[pl.ds(pl.multiple_of(hd * 256, 256), 256), :],
        loc_sem.at[7],
    )
    w_local.start()

    m_s[...] = jnp.full_like(m_s, LOW)
    l_s[...] = jnp.zeros_like(l_s)
    acc[...] = jnp.zeros_like(acc)

    def wait_part(g, k):
        remote(kv.at[g, k], kv.at[g, k], ring_send.at[0], kv_recv.at[g * 2 + k], (sib, hd)).wait_recv()

    def service(code):
        @pl.when(code >= 0)
        def _():
            half = jnp.where(code >= 8, 1 - z, z)
            i = lax.rem(code, 8)
            g = block_of(half, i)
            for k in range(2):
                wait_part(g, k)
                for kind in (0, 2, 3, 6):
                    @pl.when(i == kind)
                    def _(kind=kind):
                        for cp in sends_of(kind, half, g, k):
                            cp.start()

    def pipelined(n, scores, finish):
        state = scores(0)
        for j in range(n):
            later = scores(j + 1) if j + 1 < n else None
            finish(j, state)
            state = later

    def absorb(qh, rows, sc, val):
        mo = m_s[qh, rows, :]
        mn = jnp.maximum(mo, jnp.max(sc, axis=-1, keepdims=True))
        m_s[qh, rows, :] = mn
        return sc, mo, mn, val

    def settle(qh, rows, state):
        sc, mo, mn, val = state
        p = jnp.exp2((sc - mn[:, :1]) * SCALE)
        sh = jnp.exp2((mo - mn) * SCALE)
        ls = p[:, 0:128]
        for u in range(1, p.shape[1] // 128):
            ls = ls + p[:, u * 128:(u + 1) * 128]
        l_s[qh, rows, :] = l_s[qh, rows, :] * sh + ls
        acc[qh, rows, :] = acc[qh, rows, :] * sh + jnp.dot(
            p.astype(jnp.bfloat16), val(), preferred_element_type=jnp.float32
        )

    def attend(qh, g):
        gq = seq_of(qh, x, c)

        @pl.when(g < gq)
        def _():
            def scores(j):
                rows = pl.ds(j * CHUNK, CHUNK)
                return absorb(
                    qh, rows, dot_nt(q[qh, rows, :], kv[g, 0, :, :]), lambda: kv[g, 1, :, :]
                )

            pipelined(ROWS // CHUNK, scores, lambda j, st: settle(qh, pl.ds(j * CHUNK, CHUNK), st))

        @pl.when(g == gq)
        def _():
            def scores(j):
                rows = pl.ds(j * CHUNK, CHUNK)
                n = (j + 1) * CHUNK
                sc = dot_nt(q[qh, rows, :], kv[g, 0, 0:n, :])
                last = sc[:, n - CHUNK:]
                ok = lax.broadcasted_iota(jnp.int32, (CHUNK, CHUNK), 1) <= lax.broadcasted_iota(
                    jnp.int32, (CHUNK, CHUNK), 0
                )
                last = jnp.where(ok, last, LOW)
                if j:
                    last = jnp.concatenate([sc[:, : n - CHUNK], last], axis=1)
                return absorb(qh, rows, last, lambda: kv[g, 1, 0:n, :])

            pipelined(ROWS // CHUNK, scores, lambda j, st: settle(qh, pl.ds(j * CHUNK, CHUNK), st))

    def mem_copy(r, e):
        dst = seq_of(e, (r // 2) % 4, lax.rem(r, 2))
        at = (r // 8) * 16 + s
        return dst, at

    def pair(at):
        return mem.at[pl.ds(at * 2, 2)]

    def mem_remote(r, e):
        dst, at = mem_copy(r, e)
        return remote(
            stage.at[r, e], pair(at), mem_send.at[r * 2 + e], mem_recv.at[at], (dst, hd)
        )

    def hot_copies(n):
        at = pl.ds(4 * n + 2 * c, 2)
        return remote(hot.at[at], hot.at[at], hot_send.at[n], hot_recv.at[n], (sib, hd))

    def head_cols(zhs, yy, zz):
        return pl.ds(pl.multiple_of(((zhs * 4 + yy) * 2 + zz) * HD, HD), HD)

    def z_send(h, n, yy, src, zhd):
        at = (h * 4 + n) * 4 + z * 2 + zh
        return remote(
            src, a_ref.at[:, head_cols(zh, yy, z)],
            zs.at[(h * 4 + n) * 2 + jnp.where(zhd == zh, 0, 1)], zr.at[at],
            (seq_of(h, x, c), zhd * 4 + y),
        )

    def z_local(h, n, yy, src):
        return pltpu.make_async_copy(src, a_ref.at[:, head_cols(zh, yy, z)], as_.at[h * 4 + n])

    def z_start(h, n, yy, src):
        z_send(h, n, yy, src, 1 - zh).start()

        @pl.when(z == h)
        def _():
            z_local(h, n, yy, src).start()

        @pl.when(z != h)
        def _():
            z_send(h, n, yy, src, zh).start()

    def z_arrived(h, n, yy):
        z_local(h, n, yy, o.at[0]).wait()
        for zz, zhs in ((h, 1 - zh), (1 - h, zh), (1 - h, 1 - zh)):
            at = (h * 4 + n) * 4 + zz * 2 + zhs
            remote(
                o.at[0], a_ref.at[:, head_cols(zhs, yy, zz)], zs.at[0], zr.at[at], (sib, hd)
            ).wait_recv()

    def z_left(h, n, yy, src):
        z_send(h, n, yy, src, 1 - zh).wait_send()

        @pl.when(z != h)
        def _():
            z_send(h, n, yy, src, zh).wait_send()

    def slab(zz, yy):
        return a_ref.at[:, pl.ds(pl.multiple_of((zz * 4 + yy) * 256, 256), 256)]

    def y_slab(h, n, zz, yy, dev):
        return remote(
            slab(zz, yy), slab(zz, yy), ys.at[h * 6 + n], yr.at[h * 8 + yy * 2 + zz], (s, dev)
        )

    def y_part(h, n, part, yy, dev, first=False):
        rows = pl.ds(part * 512, 512)
        src = o.at[h, rows] if first else ybuf.at[yy, h, rows]
        return remote(
            src, ybuf.at[yy, h, rows], ys.at[h * 6 + n], yr.at[h * 8 + yy * 2 + part], (s, dev)
        )

    def y_own(h, f, **kw):
        return [
            f(h, 0, 0, y, up, **kw), f(h, 1, 1, y, dn, **kw),
            f(h, 2, 1, y, up, **kw), f(h, 3, 0, y, dn, **kw),
        ]

    def turn(h, f):
        f(h, 0, 0, yy1, up).wait_recv()
        f(h, 4, 0, yy1, up).start()
        f(h, 0, 1, yy2, up).wait_recv()
        f(h, 5, 1, yy2, dn).start()

    def heads_start(h):
        @pl.when(c == 1)
        def _():
            for cp in y_own(h, y_part, first=True):
                cp.start()

        @pl.when(c == 0)
        def _():
            z_start(h, 0, y, o.at[h])

    def heads_mid(h):
        @pl.when((c == 0) & (z == h))
        def _():
            z_arrived(h, 0, y)
            for cp in y_own(h, y_slab):
                cp.start()

        @pl.when(c == 1)
        def _():
            turn(h, y_part)
            z_start(h, 0, y, o.at[h])

    def heads_near(h):
        @pl.when(c == 1)
        def _():
            y_part(h, 0, 1, yy1, up).wait_recv()
            z_start(h, 1, yy1, ybuf.at[yy1, h])
            y_part(h, 0, 0, yy2, up).wait_recv()
            z_start(h, 2, yy2, ybuf.at[yy2, h])

    def heads_fwd(h):
        @pl.when((c == 0) & (z == h))
        def _():
            turn(h, y_slab)

        @pl.when(c == 1)
        def _():
            y_part(h, 0, 0, yy3, up).wait_recv()
            y_part(h, 0, 1, yy3, up).wait_recv()
            z_start(h, 3, yy3, ybuf.at[yy3, h])

    def project(zz, yy):
        at = pl.ds(pl.multiple_of((zz * 4 + yy) * 256, 256), 256)

        def part(j, _):
            rows = pl.ds(pl.multiple_of(j * CHUNK, CHUNK), CHUNK)
            total[rows, :] += jnp.dot(
                a_ref[rows, at], wc[at, :], preferred_element_type=jnp.float32
            )
            return 0

        lax.fori_loop(0, ROWS // CHUNK, part, 0)

    def heads_end(h):
        @pl.when((c == 0) & (z == h))
        def _():
            project(0, y)
            project(1, y)
            project(0, yy1)
            project(1, yy2)
            for zz, yy in ((1, yy1), (0, yy2), (0, yy3), (1, yy3)):
                y_slab(h, 0, zz, yy, up).wait_recv()
                project(zz, yy)
            for cp in y_own(h, y_slab) + [y_slab(h, 4, 0, yy1, up), y_slab(h, 5, 1, yy2, dn)]:
                cp.wait_send()

        @pl.when((c == 1) & (z == h))
        def _():
            for n, yy in ((0, y), (1, yy1), (2, yy2), (3, yy3)):
                z_arrived(h, n, yy)
                project(0, yy)
                project(1, yy)

        z_left(h, 0, y, o.at[h])

        @pl.when(c == 1)
        def _():
            for n, yy in ((1, yy1), (2, yy2), (3, yy3)):
                z_left(h, n, yy, ybuf.at[yy, h])
            for cp in y_own(h, y_part, first=True):
                cp.wait_send()
            y_part(h, 4, 0, yy1, up).wait_send()
            y_part(h, 5, 1, yy2, dn).wait_send()

    def step(t, _):
        @pl.when(t == 8)
        def _():
            remote(q.at[0], q.at[1 - z], swap_send.at[3], q_recv.at[0], (zp, hd)).wait_recv()

        service(pick(t, SERVICE_A, -1))
        service(pick(t, SERVICE_B, -1))

        @pl.when(t == GATHER_AT)
        def _():
            def wait_req(i, _):
                @pl.when(i != s)
                def _():
                    remote(
                        req_ref.at[i], reqin.at[i], req_send.at[i], req_recv.at[i], (sib, hd)
                    ).wait_recv()
                return 0

            lax.fori_loop(0, 16, wait_req, 0)
            swaps[2].wait_recv()
            for cp in loc[3:]:
                cp.wait()
            a = pltpu.make_async_copy(reqin, reqs, loc_sem.at[8])
            b = pltpu.make_async_copy(infoin, infos.at[1 - z], loc_sem.at[9])
            a.start()
            b.start()
            a.wait()
            b.wait()

            def gather(r, _):
                for b2 in range(2):
                    b = reqs[r, 0, b2]
                    kr = mk[b]
                    vr = mv[b]
                    for e in range(2):
                        cols = slice(e * HD, (e + 1) * HD)
                        stage[r, e, b2, 0] = kr[:, cols]
                        stage[r, e, b2, 1] = vr[:, cols]
                return 0

            lax.fori_loop(0, 16, gather, 0)

        @pl.when((t == MEM_NEAR) | (t == MEM_FAR))
        def _():
            def send(i, _):
                r = lax.rem(i + s + 1, 16)
                e = jnp.where(t == MEM_NEAR, z, 1 - z)
                dst, at = mem_copy(r, e)

                @pl.when(dst == s)
                def _():
                    pltpu.make_async_copy(stage.at[r, e], pair(at), mem_recv.at[at]).start()

                @pl.when(dst != s)
                def _():
                    mem_remote(r, e).start()
                return 0

            lax.fori_loop(0, 16, send, 0)

        native = t < 8
        u = t - 8
        qh = jnp.where(native, z, jnp.where(z == 0, 1, lax.rem(t, 2)))
        half = jnp.where(native, z, jnp.where((z == 0) & (u >= 8), 1, 0))
        i = jnp.where(native, t, jnp.where(z == 0, lax.rem(t, 8), u // 2))
        attend(qh, block_of(half, i))
        return 0

    loc[2].wait()
    lax.fori_loop(0, STEPS, step, 0)

    def wait_mem(i, _):
        own = lax.rem(i, 16) == s

        @pl.when(jnp.logical_not(own))
        def _():
            remote(
                stage.at[0, 0], pair(i), mem_send.at[0], mem_recv.at[i], (sib, hd)
            ).wait_recv()

        @pl.when(own)
        def _():
            pltpu.make_async_copy(stage.at[0, 0], pair(i), mem_recv.at[i]).wait()
        return 0

    lax.fori_loop(0, 32, wait_mem, 0)
    ho = infos[z, 0, 40]
    for n in range(2):
        for b2 in range(2):
            hot[4 * n + 2 * c + b2] = mem[(n * 16 + ho) * 2 + b2]
        hot_copies(n).start()
    for n in range(2):
        at = pl.ds(4 * n + 2 * (1 - c), 2)
        remote(hot.at[at], hot.at[at], hot_send.at[n], hot_recv.at[n], (sib, hd)).wait_recv()
    for j in range(8):
        mem[64 + j] = hot[j]

    def mem_group(i, _):
        qh = i // 4
        j = lax.rem(i, 4)
        for e in range(TOPB):
            code = infos[qh, 0, j * TOPB + e]
            kc[e * BLOCK:(e + 1) * BLOCK, :] = mem[code, 0]
            vc[e * BLOCK:(e + 1) * BLOCK, :] = mem[code, 1]
        rows = pl.ds(pl.multiple_of(j * GROUP, GROUP), GROUP)
        st = absorb(qh, rows, dot_nt(q[qh, rows, :], kc[...]), lambda: vc[...])
        settle(qh, rows, st)
        o[qh, rows, :] = (
            acc[qh, rows, :] / jnp.sum(l_s[qh, rows, :], axis=-1, keepdims=True)
        ).astype(jnp.bfloat16)
        return 0

    lax.fori_loop(0, 4, mem_group, 0)
    heads_start(0)
    lax.fori_loop(4, 8, mem_group, 0)
    heads_start(1)

    def wait_w(i, _):
        @pl.when(i != hd)
        def _():
            rows = pl.ds(pl.multiple_of(i * 256, 256), 256)
            remote(
                w_hbm.at[:, pl.ds(0, 512)], wc.at[rows, :], w_send.at[i], w_recv.at[i], (sib, hd)
            ).wait_recv()
        return 0

    lax.fori_loop(0, 8, wait_w, 0)
    w_local.wait()
    total[...] = jnp.zeros_like(total)
    heads_mid(0)
    heads_mid(1)
    heads_near(0)
    heads_near(1)
    heads_fwd(0)
    heads_fwd(1)
    heads_end(0)
    heads_end(1)

    for cp in swaps:
        cp.wait_send()
    for half in (0, 1):
        for kind in (0, 2, 3, 6):
            for k in range(2):
                for cp in sends_of(kind, half, s, k):
                    cp.wait_send()
    for n in range(2):
        hot_copies(n).wait_send()

    def drain_req(i, _):
        @pl.when(i != s)
        def _():
            req_copy(i).wait_send()
        return 0

    lax.fori_loop(0, 16, drain_req, 0)

    def drain_mem(i, _):
        dst, _at = mem_copy(i // 2, lax.rem(i, 2))

        @pl.when(dst != s)
        def _():
            mem_remote(i // 2, lax.rem(i, 2)).wait_send()
        return 0

    lax.fori_loop(0, 32, drain_mem, 0)

    def drain_w(i, _):
        @pl.when(i != hd)
        def _():
            w_copy(i).wait_send()
        return 0

    lax.fori_loop(0, 8, drain_w, 0)
    out_ref[...] = total[...].astype(jnp.bfloat16)


def attention(q, k, v, mk, mv, req, info, w):
    any_ = pl.BlockSpec(memory_space=pl.ANY)
    vm = pl.BlockSpec(memory_space=pltpu.VMEM)
    b16 = jnp.bfloat16
    dma = pltpu.SemaphoreType.DMA
    return pl.pallas_call(
        attention_kernel,
        out_shape=jax.ShapeDtypeStruct((ROWS, 512), b16),
        in_specs=[any_] * 5 + [vm, vm, any_],
        out_specs=vm,
        scratch_shapes=[
            pltpu.VMEM((2, ROWS, HD), b16),
            pltpu.VMEM((16, 2, ROWS, HD), b16),
            pltpu.VMEM((2, ROWS, HD), jnp.float32),
            pltpu.VMEM((2, ROWS, HD), jnp.float32),
            pltpu.VMEM((2, ROWS, HD), jnp.float32),
            pltpu.VMEM((64, BLOCK, 2 * HD), b16),
            pltpu.VMEM((64, BLOCK, 2 * HD), b16),
            pltpu.VMEM((16, 2, 2, 2, BLOCK, HD), b16),
            pltpu.VMEM((72, 2, BLOCK, HD), b16),
            pltpu.VMEM((8, 2, BLOCK, HD), b16),
            pltpu.VMEM((TOPB * BLOCK, HD), b16),
            pltpu.VMEM((TOPB * BLOCK, HD), b16),
            pltpu.VMEM((2, ROWS, HD), b16),
            pltpu.VMEM((4, 2, ROWS, HD), b16),
            pltpu.VMEM((ROWS, 2048), b16),
            pltpu.VMEM((2048, 512), b16),
            pltpu.VMEM((ROWS, 512), jnp.float32),
            pltpu.VMEM((16, 8, 128), jnp.int32),
            pltpu.VMEM((8, 128), jnp.int32),
            pltpu.SMEM((16, 8, 128), jnp.int32),
            pltpu.SMEM((2, 8, 128), jnp.int32),
            dma((10,)),
            dma((32,)),
            dma((28,)),
            dma((4,)),
            dma((1,)),
            dma((1,)),
            dma((16,)),
            dma((16,)),
            dma((32,)),
            dma((32,)),
            dma((2,)),
            dma((2,)),
            dma((8,)),
            dma((8,)),
            dma((16,)),
            dma((32,)),
            dma((12,)),
            dma((16,)),
            dma((8,)),
        ],
        compiler_params=pltpu.CompilerParams(
            collective_id=0, has_side_effects=True, vmem_limit_bytes=56 << 20
        ),
        name="attention",
    )(q, k, v, mk, mv, req, info, w)


def tables(block_index):
    z = lax.axis_index("seq") // 8
    w = block_index.reshape(-1)
    holder = w // 64
    local = w - holder * 64
    owners = jnp.arange(16, dtype=jnp.int32)
    n = jnp.arange(32, dtype=jnp.int32)
    same = holder[:, None] == holder[None, :]
    count = jnp.sum(same.astype(jnp.int32), axis=1)
    place = jnp.sum((same & (n[None, :] < n[:, None])).astype(jnp.int32), axis=1)
    is_hot = count == TOPB
    rank = jnp.sum((same & (local[None, :] < local[:, None])).astype(jnp.int32), axis=1)
    lanes = jnp.arange(128, dtype=jnp.int32)
    mine = z * 2 + lax.axis_index("seq") % 2
    slot = jnp.where(is_hot, rank - 2 * mine, place)
    hit = (holder[:, None, None] == owners[None, :, None]) & (
        slot[:, None, None] == lanes[None, None, :]
    ) & (lanes < 2)[None, None, :]
    req = jnp.sum(jnp.where(hit, local[:, None, None], 0), axis=0)
    code = jnp.where(is_hot, 64 + rank, (z * 16 + holder) * 2 + place)
    at_code = n[:, None] == lanes[None, :]
    at_hot = is_hot[:, None] & ((rank + 32)[:, None] == lanes[None, :])
    at_owner = (is_hot & (rank == 0))[:, None] & (lanes == 40)[None, :]
    info = jnp.sum(
        jnp.where(at_code, code[:, None], 0)
        + jnp.where(at_hot, local[:, None], 0)
        + jnp.where(at_owner, holder[:, None], 0),
        axis=0,
    )
    return (
        jnp.broadcast_to(req[:, None, :], (16, 8, 128)),
        jnp.broadcast_to(info[None, :], (8, 128)),
    )


def shards(q, k, v, mk, mv, block_index, w):
    req, info = tables(block_index)
    return attention(
        q, k, v, mk.reshape(-1, BLOCK, 2 * HD), mv.reshape(-1, BLOCK, 2 * HD), req, info, w
    )


def solution(mesh):
    return jax.shard_map(
        shards,
        mesh=mesh,
        in_specs=(
            P("seq", "head"), P("seq", "head"), P("seq", "head"), P("seq", "head"),
            P("seq", "head"), P("seq", None), P("head", None),
        ),
        out_specs=P("seq", "head"),
        check_vma=False,
    )
```

```python
import functools
import math

import jax
import jax.numpy as jnp
from jax import lax
from jax.experimental import pallas as pl
from jax.experimental.pallas import tpu as pltpu
from jax.sharding import PartitionSpec as P

MESH = pl.DeviceIdType.MESH
HD = 128
GROUP = 256
BLOCK = 64
TOPB = 8
ROWS = 1024
CHUNK = 256
SCALE = math.log2(math.e) / math.sqrt(HD)
LOW = -1e30
STEPS = 24
GATHER_AT = 1
MEM_NEAR = 9
MEM_FAR = 12


def where_am_i():
    s = lax.axis_index("seq")
    hd = lax.axis_index("head")
    return s, hd, s // 8, (s // 2) % 4, s % 2, hd // 4, hd % 4


def seq_of(z, x, c):
    return z * 8 + x * 2 + c


def dot_nt(a, b):
    return lax.dot_general(a, b, (((1,), (1,)), ((), ())), preferred_element_type=jnp.float32)


def pick(t, table, default):
    out = default
    for k, v in table.items():
        out = jnp.where(t == k, v, out)
    return out


def remote(src, dst, ss, rs, dev):
    return pltpu.make_async_remote_copy(
        src_ref=src, dst_ref=dst, send_sem=ss, recv_sem=rs, device_id=dev, device_id_type=MESH
    )


DXS = (0, 0, 3, 1, 3, 1, 2, 2)
SIBS = (0, 1, 0, 0, 1, 1, 0, 1)
SERVICE_A = {1: 1, 2: 2, 3: 8, 4: 4, 5: 5, 6: 6, 7: 7, 10: 9, 12: 10, 16: 12, 18: 13, 20: 14, 22: 15}
SERVICE_B = {2: 3, 12: 11}


def attention_kernel(
    q_hbm, k_hbm, v_hbm, mk_hbm, mv_hbm, req_ref, info_ref, w_hbm,
    out_ref,
    q, kv, m_s, l_s, acc, mk, mv, stage, mem, hot, kc, vc, o, ybuf, a_ref, wc, total,
    reqin, infoin, reqs, infos,
    loc_sem, kv_recv, ring_send, swap_send, q_recv, info_recv,
    req_send, req_recv, mem_send, mem_recv, hot_send, hot_recv, w_send, w_recv,
    zs, zr, ys, yr, as_,
):
    s, hd, z, x, c, zh, y = where_am_i()
    up = zh * 4 + lax.rem(y + 1, 4)
    dn = zh * 4 + lax.rem(y + 3, 4)
    yy1 = lax.rem(y + 3, 4)
    yy2 = lax.rem(y + 1, 4)
    yy3 = lax.rem(y + 2, 4)
    zp = seq_of(1 - z, x, c)
    sib = seq_of(z, x, 1 - c)
    xr = seq_of(z, lax.rem(x + 1, 4), c)
    xl = seq_of(z, lax.rem(x + 3, 4), c)

    mine = pl.ds(pl.multiple_of(z * HD, HD), HD)
    theirs = pl.ds(pl.multiple_of((1 - z) * HD, HD), HD)
    loc = [
        pltpu.make_async_copy(k_hbm.at[:, mine], kv.at[s, 0], loc_sem.at[0]),
        pltpu.make_async_copy(v_hbm.at[:, mine], kv.at[s, 1], loc_sem.at[1]),
        pltpu.make_async_copy(q_hbm.at[:, mine], q.at[z], loc_sem.at[2]),
        pltpu.make_async_copy(mk_hbm, mk, loc_sem.at[3]),
        pltpu.make_async_copy(mv_hbm, mv, loc_sem.at[4]),
        pltpu.make_async_copy(info_ref, infos.at[z], loc_sem.at[5]),
        pltpu.make_async_copy(req_ref.at[s], reqin.at[s], loc_sem.at[6]),
    ]
    for cp in loc:
        cp.start()

    bar = pltpu.get_barrier_semaphore()

    def w_target(i):
        same = (i // 4) == zh
        zd = jnp.where(same, z, 1 - z)
        return (seq_of(zd, x, c), i)

    def greet(i, _):
        @pl.when(i != s)
        def _():
            pl.semaphore_signal(bar, inc=1, device_id=(i, hd), device_id_type=MESH)
        return 0

    lax.fori_loop(0, 16, greet, 0)

    def greet_w(i, _):
        @pl.when(i != hd)
        def _():
            pl.semaphore_signal(bar, inc=1, device_id=w_target(i), device_id_type=MESH)
        return 0

    lax.fori_loop(0, 8, greet_w, 0)
    pl.semaphore_signal(bar, inc=1, device_id=(s, (1 - zh) * 4 + y), device_id_type=MESH)
    pl.semaphore_wait(bar, 23)

    swaps = [
        remote(k_hbm.at[:, theirs], kv.at[s, 0], swap_send.at[0], kv_recv.at[s * 2], (zp, hd)),
        remote(v_hbm.at[:, theirs], kv.at[s, 1], swap_send.at[1], kv_recv.at[s * 2 + 1], (zp, hd)),
        remote(info_ref, infoin, swap_send.at[2], info_recv.at[0], (zp, hd)),
        remote(q_hbm.at[:, theirs], q.at[z], swap_send.at[3], q_recv.at[0], (zp, hd)),
    ]
    swaps[2].start()

    def req_copy(i):
        return remote(req_ref.at[i], reqin.at[s], req_send.at[i], req_recv.at[s], (i, hd))

    def send_req(i, _):
        @pl.when(i != s)
        def _():
            req_copy(i).start()
        return 0

    lax.fori_loop(0, 16, send_req, 0)
    swaps[0].start()
    swaps[1].start()

    def ring_copy(half, n, g, k, dev):
        return remote(
            kv.at[g, k], kv.at[g, k], ring_send.at[half * 14 + n], kv_recv.at[g * 2 + k], (dev, hd)
        )

    def sends_of(kind, half, g, k):
        if kind == 0:
            n = 3 * k
            return [
                ring_copy(half, n, g, k, xr), ring_copy(half, n + 1, g, k, xl),
                ring_copy(half, n + 2, g, k, sib),
            ]
        if kind == 2:
            on = [ring_copy(half, 6, g, 0, xr)] if k == 0 else []
            return on + [ring_copy(half, 7 + k, g, k, sib)]
        if kind == 3:
            on = [ring_copy(half, 9, g, 1, xl)] if k == 1 else []
            return on + [ring_copy(half, 10 + k, g, k, sib)]
        return [ring_copy(half, 12 + k, g, k, sib)]

    def block_of(half, i):
        dx = pick(i, dict(enumerate(DXS)), 0)
        sb = pick(i, dict(enumerate(SIBS)), 0)
        return seq_of(half, lax.rem(x + dx, 4), jnp.where(sb == 1, 1 - c, c))

    for k in range(2):
        loc[k].wait()
        for cp in sends_of(0, z, s, k):
            cp.start()
    swaps[3].start()

    def w_copy(i):
        cols = pl.ds(pl.multiple_of(i * 512, 512), 512)
        rows = pl.ds(pl.multiple_of(hd * 256, 256), 256)
        return remote(
            w_hbm.at[:, cols], wc.at[rows, :], w_send.at[i], w_recv.at[hd], w_target(i)
        )

    def send_w(i, _):
        @pl.when(i != hd)
        def _():
            w_copy(i).start()
        return 0

    lax.fori_loop(0, 8, send_w, 0)
    w_local = pltpu.make_async_copy(
        w_hbm.at[:, pl.ds(pl.multiple_of(hd * 512, 512), 512)],
        wc.at[pl.ds(pl.multiple_of(hd * 256, 256), 256), :],
        loc_sem.at[7],
    )
    w_local.start()

    m_s[...] = jnp.full_like(m_s, LOW)
    l_s[...] = jnp.zeros_like(l_s)
    acc[...] = jnp.zeros_like(acc)

    def wait_part(g, k):
        remote(kv.at[g, k], kv.at[g, k], ring_send.at[0], kv_recv.at[g * 2 + k], (sib, hd)).wait_recv()

    def service(code):
        @pl.when(code >= 0)
        def _():
            half = jnp.where(code >= 8, 1 - z, z)
            i = lax.rem(code, 8)
            g = block_of(half, i)
            for k in range(2):
                wait_part(g, k)
                for kind in (0, 2, 3, 6):
                    @pl.when(i == kind)
                    def _(kind=kind):
                        for cp in sends_of(kind, half, g, k):
                            cp.start()

    def pipelined(n, scores, finish):
        state = scores(0)
        for j in range(n):
            later = scores(j + 1) if j + 1 < n else None
            finish(j, state)
            state = later

    def absorb(qh, rows, sc, val):
        mo = m_s[qh, rows, :]
        mn = jnp.maximum(mo, jnp.max(sc, axis=-1, keepdims=True))
        m_s[qh, rows, :] = mn
        return sc, mo, mn, val

    def settle(qh, rows, state):
        sc, mo, mn, val = state
        p = jnp.exp2((sc - mn[:, :1]) * SCALE)
        sh = jnp.exp2((mo - mn) * SCALE)
        ls = p[:, 0:128]
        for u in range(1, p.shape[1] // 128):
            ls = ls + p[:, u * 128:(u + 1) * 128]
        l_s[qh, rows, :] = l_s[qh, rows, :] * sh + ls
        acc[qh, rows, :] = acc[qh, rows, :] * sh + jnp.dot(
            p.astype(jnp.bfloat16), val(), preferred_element_type=jnp.float32
        )

    def attend(qh, g):
        gq = seq_of(qh, x, c)

        @pl.when(g < gq)
        def _():
            def scores(j):
                rows = pl.ds(j * CHUNK, CHUNK)
                return absorb(
                    qh, rows, dot_nt(q[qh, rows, :], kv[g, 0, :, :]), lambda: kv[g, 1, :, :]
                )

            pipelined(ROWS // CHUNK, scores, lambda j, st: settle(qh, pl.ds(j * CHUNK, CHUNK), st))

        @pl.when(g == gq)
        def _():
            def scores(j):
                rows = pl.ds(j * CHUNK, CHUNK)
                n = (j + 1) * CHUNK
                sc = dot_nt(q[qh, rows, :], kv[g, 0, 0:n, :])
                last = sc[:, n - CHUNK:]
                ok = lax.broadcasted_iota(jnp.int32, (CHUNK, CHUNK), 1) <= lax.broadcasted_iota(
                    jnp.int32, (CHUNK, CHUNK), 0
                )
                last = jnp.where(ok, last, LOW)
                if j:
                    last = jnp.concatenate([sc[:, : n - CHUNK], last], axis=1)
                return absorb(qh, rows, last, lambda: kv[g, 1, 0:n, :])

            pipelined(ROWS // CHUNK, scores, lambda j, st: settle(qh, pl.ds(j * CHUNK, CHUNK), st))

    def mem_copy(r, e):
        dst = seq_of(e, (r // 2) % 4, lax.rem(r, 2))
        at = (r // 8) * 16 + s
        return dst, at

    def pair(at):
        return mem.at[pl.ds(at * 2, 2)]

    def mem_remote(r, e):
        dst, at = mem_copy(r, e)
        return remote(
            stage.at[r, e], pair(at), mem_send.at[r * 2 + e], mem_recv.at[at], (dst, hd)
        )

    def hot_copies(n):
        at = pl.ds(4 * n + 2 * c, 2)
        return remote(hot.at[at], hot.at[at], hot_send.at[n], hot_recv.at[n], (sib, hd))

    def head_cols(zhs, yy, zz):
        return pl.ds(pl.multiple_of(((zhs * 4 + yy) * 2 + zz) * HD, HD), HD)

    def z_send(h, n, yy, src, zhd):
        at = (h * 4 + n) * 4 + z * 2 + zh
        return remote(
            src, a_ref.at[:, head_cols(zh, yy, z)],
            zs.at[(h * 4 + n) * 2 + jnp.where(zhd == zh, 0, 1)], zr.at[at],
            (seq_of(h, x, c), zhd * 4 + y),
        )

    def z_local(h, n, yy, src):
        return pltpu.make_async_copy(src, a_ref.at[:, head_cols(zh, yy, z)], as_.at[h * 4 + n])

    def z_start(h, n, yy, src):
        z_send(h, n, yy, src, 1 - zh).start()

        @pl.when(z == h)
        def _():
            z_local(h, n, yy, src).start()

        @pl.when(z != h)
        def _():
            z_send(h, n, yy, src, zh).start()

    def z_arrived(h, n, yy):
        z_local(h, n, yy, o.at[0]).wait()
        for zz, zhs in ((h, 1 - zh), (1 - h, zh), (1 - h, 1 - zh)):
            at = (h * 4 + n) * 4 + zz * 2 + zhs
            remote(
                o.at[0], a_ref.at[:, head_cols(zhs, yy, zz)], zs.at[0], zr.at[at], (sib, hd)
            ).wait_recv()

    def z_left(h, n, yy, src):
        z_send(h, n, yy, src, 1 - zh).wait_send()

        @pl.when(z != h)
        def _():
            z_send(h, n, yy, src, zh).wait_send()

    def slab(zz, yy):
        return a_ref.at[:, pl.ds(pl.multiple_of((zz * 4 + yy) * 256, 256), 256)]

    def y_slab(h, n, zz, yy, dev):
        return remote(
            slab(zz, yy), slab(zz, yy), ys.at[h * 6 + n], yr.at[h * 8 + yy * 2 + zz], (s, dev)
        )

    def y_part(h, n, part, yy, dev, first=False):
        rows = pl.ds(part * 512, 512)
        src = o.at[h, rows] if first else ybuf.at[yy, h, rows]
        return remote(
            src, ybuf.at[yy, h, rows], ys.at[h * 6 + n], yr.at[h * 8 + yy * 2 + part], (s, dev)
        )

    def y_own(h, f, **kw):
        return [
            f(h, 0, 0, y, up, **kw), f(h, 1, 1, y, dn, **kw),
            f(h, 2, 1, y, up, **kw), f(h, 3, 0, y, dn, **kw),
        ]

    def turn(h, f):
        f(h, 0, 0, yy1, up).wait_recv()
        f(h, 4, 0, yy1, up).start()
        f(h, 0, 1, yy2, up).wait_recv()
        f(h, 5, 1, yy2, dn).start()

    def heads_start(h):
        @pl.when(c == 1)
        def _():
            for cp in y_own(h, y_part, first=True):
                cp.start()

        @pl.when(c == 0)
        def _():
            z_start(h, 0, y, o.at[h])

    def heads_mid(h):
        @pl.when((c == 0) & (z == h))
        def _():
            z_arrived(h, 0, y)
            for cp in y_own(h, y_slab):
                cp.start()

        @pl.when(c == 1)
        def _():
            turn(h, y_part)
            z_start(h, 0, y, o.at[h])

    def heads_near(h):
        @pl.when(c == 1)
        def _():
            y_part(h, 0, 1, yy1, up).wait_recv()
            z_start(h, 1, yy1, ybuf.at[yy1, h])
            y_part(h, 0, 0, yy2, up).wait_recv()
            z_start(h, 2, yy2, ybuf.at[yy2, h])

    def heads_fwd(h):
        @pl.when((c == 0) & (z == h))
        def _():
            turn(h, y_slab)

        @pl.when(c == 1)
        def _():
            y_part(h, 0, 0, yy3, up).wait_recv()
            y_part(h, 0, 1, yy3, up).wait_recv()
            z_start(h, 3, yy3, ybuf.at[yy3, h])

    def project(zz, yy):
        at = pl.ds(pl.multiple_of((zz * 4 + yy) * 256, 256), 256)

        def part(j, _):
            rows = pl.ds(pl.multiple_of(j * CHUNK, CHUNK), CHUNK)
            total[rows, :] += jnp.dot(
                a_ref[rows, at], wc[at, :], preferred_element_type=jnp.float32
            )
            return 0

        lax.fori_loop(0, ROWS // CHUNK, part, 0)

    def heads_end(h):
        @pl.when((c == 0) & (z == h))
        def _():
            project(0, y)
            project(1, y)
            project(0, yy1)
            project(1, yy2)
            for zz, yy in ((1, yy1), (0, yy2), (0, yy3), (1, yy3)):
                y_slab(h, 0, zz, yy, up).wait_recv()
                project(zz, yy)
            for cp in y_own(h, y_slab) + [y_slab(h, 4, 0, yy1, up), y_slab(h, 5, 1, yy2, dn)]:
                cp.wait_send()

        @pl.when((c == 1) & (z == h))
        def _():
            for n, yy in ((0, y), (1, yy1), (2, yy2), (3, yy3)):
                z_arrived(h, n, yy)
                project(0, yy)
                project(1, yy)

        z_left(h, 0, y, o.at[h])

        @pl.when(c == 1)
        def _():
            for n, yy in ((1, yy1), (2, yy2), (3, yy3)):
                z_left(h, n, yy, ybuf.at[yy, h])
            for cp in y_own(h, y_part, first=True):
                cp.wait_send()
            y_part(h, 4, 0, yy1, up).wait_send()
            y_part(h, 5, 1, yy2, dn).wait_send()

    def step(t, _):
        @pl.when(t == 8)
        def _():
            remote(q.at[0], q.at[1 - z], swap_send.at[3], q_recv.at[0], (zp, hd)).wait_recv()

        service(pick(t, SERVICE_A, -1))
        service(pick(t, SERVICE_B, -1))

        @pl.when(t == GATHER_AT)
        def _():
            def wait_req(i, _):
                @pl.when(i != s)
                def _():
                    remote(
                        req_ref.at[i], reqin.at[i], req_send.at[i], req_recv.at[i], (sib, hd)
                    ).wait_recv()
                return 0

            lax.fori_loop(0, 16, wait_req, 0)
            swaps[2].wait_recv()
            for cp in loc[3:]:
                cp.wait()
            a = pltpu.make_async_copy(reqin, reqs, loc_sem.at[8])
            b = pltpu.make_async_copy(infoin, infos.at[1 - z], loc_sem.at[9])
            a.start()
            b.start()
            a.wait()
            b.wait()

            def gather(r, _):
                for b2 in range(2):
                    b = reqs[r, 0, b2]
                    kr = mk[b]
                    vr = mv[b]
                    for e in range(2):
                        cols = slice(e * HD, (e + 1) * HD)
                        stage[r, e, b2, 0] = kr[:, cols]
                        stage[r, e, b2, 1] = vr[:, cols]
                return 0

            lax.fori_loop(0, 16, gather, 0)

        @pl.when((t == MEM_NEAR) | (t == MEM_FAR))
        def _():
            def send(i, _):
                r = lax.rem(i + s + 1, 16)
                e = jnp.where(t == MEM_NEAR, z, 1 - z)
                dst, at = mem_copy(r, e)

                @pl.when(dst == s)
                def _():
                    pltpu.make_async_copy(stage.at[r, e], pair(at), mem_recv.at[at]).start()

                @pl.when(dst != s)
                def _():
                    mem_remote(r, e).start()
                return 0

            lax.fori_loop(0, 16, send, 0)

        native = t < 8
        u = t - 8
        qh = jnp.where(native, z, jnp.where(z == 0, 1, lax.rem(t, 2)))
        half = jnp.where(native, z, jnp.where((z == 0) & (u >= 8), 1, 0))
        i = jnp.where(native, t, jnp.where(z == 0, lax.rem(t, 8), u // 2))
        attend(qh, block_of(half, i))
        return 0

    loc[2].wait()
    lax.fori_loop(0, STEPS, step, 0)

    def wait_mem(i, _):
        own = lax.rem(i, 16) == s

        @pl.when(jnp.logical_not(own))
        def _():
            remote(
                stage.at[0, 0], pair(i), mem_send.at[0], mem_recv.at[i], (sib, hd)
            ).wait_recv()

        @pl.when(own)
        def _():
            pltpu.make_async_copy(stage.at[0, 0], pair(i), mem_recv.at[i]).wait()
        return 0

    lax.fori_loop(0, 32, wait_mem, 0)
    ho = infos[z, 0, 40]
    for n in range(2):
        for b2 in range(2):
            hot[4 * n + 2 * c + b2] = mem[(n * 16 + ho) * 2 + b2]
        hot_copies(n).start()
    for n in range(2):
        at = pl.ds(4 * n + 2 * (1 - c), 2)
        remote(hot.at[at], hot.at[at], hot_send.at[n], hot_recv.at[n], (sib, hd)).wait_recv()
    for j in range(8):
        mem[64 + j] = hot[j]

    def mem_groups(i, _):
        qh = i // 2
        for b2 in range(2):
            j = lax.rem(i, 2) * 2 + b2
            for e in range(TOPB):
                code = infos[qh, 0, j * TOPB + e]
                kc[b2, e * BLOCK:(e + 1) * BLOCK, :] = mem[code, 0]
                vc[b2, e * BLOCK:(e + 1) * BLOCK, :] = mem[code, 1]

        def rows_of(b2):
            return pl.ds(pl.multiple_of((lax.rem(i, 2) * 2 + b2) * GROUP, GROUP), GROUP)

        def scores(b2):
            rows = rows_of(b2)
            return absorb(qh, rows, dot_nt(q[qh, rows, :], kc[b2]), lambda: vc[b2])

        def finish(b2, st):
            rows = rows_of(b2)
            settle(qh, rows, st)
            o[qh, rows, :] = (
                acc[qh, rows, :] / jnp.sum(l_s[qh, rows, :], axis=-1, keepdims=True)
            ).astype(jnp.bfloat16)

        pipelined(2, scores, finish)
        return 0

    lax.fori_loop(0, 2, mem_groups, 0)
    heads_start(0)
    lax.fori_loop(2, 4, mem_groups, 0)
    heads_start(1)

    def wait_w(i, _):
        @pl.when(i != hd)
        def _():
            rows = pl.ds(pl.multiple_of(i * 256, 256), 256)
            remote(
                w_hbm.at[:, pl.ds(0, 512)], wc.at[rows, :], w_send.at[i], w_recv.at[i], (sib, hd)
            ).wait_recv()
        return 0

    lax.fori_loop(0, 8, wait_w, 0)
    w_local.wait()
    total[...] = jnp.zeros_like(total)
    heads_mid(0)
    heads_mid(1)
    heads_near(0)
    heads_near(1)
    heads_fwd(0)
    heads_fwd(1)
    heads_end(0)
    heads_end(1)

    for cp in swaps:
        cp.wait_send()
    for half in (0, 1):
        for kind in (0, 2, 3, 6):
            for k in range(2):
                for cp in sends_of(kind, half, s, k):
                    cp.wait_send()
    for n in range(2):
        hot_copies(n).wait_send()

    def drain_req(i, _):
        @pl.when(i != s)
        def _():
            req_copy(i).wait_send()
        return 0

    lax.fori_loop(0, 16, drain_req, 0)

    def drain_mem(i, _):
        dst, _at = mem_copy(i // 2, lax.rem(i, 2))

        @pl.when(dst != s)
        def _():
            mem_remote(i // 2, lax.rem(i, 2)).wait_send()
        return 0

    lax.fori_loop(0, 32, drain_mem, 0)

    def drain_w(i, _):
        @pl.when(i != hd)
        def _():
            w_copy(i).wait_send()
        return 0

    lax.fori_loop(0, 8, drain_w, 0)
    out_ref[...] = total[...].astype(jnp.bfloat16)


def attention(q, k, v, mk, mv, req, info, w):
    any_ = pl.BlockSpec(memory_space=pl.ANY)
    vm = pl.BlockSpec(memory_space=pltpu.VMEM)
    b16 = jnp.bfloat16
    dma = pltpu.SemaphoreType.DMA
    return pl.pallas_call(
        attention_kernel,
        out_shape=jax.ShapeDtypeStruct((ROWS, 512), b16),
        in_specs=[any_] * 5 + [vm, vm, any_],
        out_specs=vm,
        scratch_shapes=[
            pltpu.VMEM((2, ROWS, HD), b16),
            pltpu.VMEM((16, 2, ROWS, HD), b16),
            pltpu.VMEM((2, ROWS, HD), jnp.float32),
            pltpu.VMEM((2, ROWS, HD), jnp.float32),
            pltpu.VMEM((2, ROWS, HD), jnp.float32),
            pltpu.VMEM((64, BLOCK, 2 * HD), b16),
            pltpu.VMEM((64, BLOCK, 2 * HD), b16),
            pltpu.VMEM((16, 2, 2, 2, BLOCK, HD), b16),
            pltpu.VMEM((72, 2, BLOCK, HD), b16),
            pltpu.VMEM((8, 2, BLOCK, HD), b16),
            pltpu.VMEM((2, TOPB * BLOCK, HD), b16),
            pltpu.VMEM((2, TOPB * BLOCK, HD), b16),
            pltpu.VMEM((2, ROWS, HD), b16),
            pltpu.VMEM((4, 2, ROWS, HD), b16),
            pltpu.VMEM((ROWS, 2048), b16),
            pltpu.VMEM((2048, 512), b16),
            pltpu.VMEM((ROWS, 512), jnp.float32),
            pltpu.VMEM((16, 8, 128), jnp.int32),
            pltpu.VMEM((8, 128), jnp.int32),
            pltpu.SMEM((16, 8, 128), jnp.int32),
            pltpu.SMEM((2, 8, 128), jnp.int32),
            dma((10,)),
            dma((32,)),
            dma((28,)),
            dma((4,)),
            dma((1,)),
            dma((1,)),
            dma((16,)),
            dma((16,)),
            dma((32,)),
            dma((32,)),
            dma((2,)),
            dma((2,)),
            dma((8,)),
            dma((8,)),
            dma((16,)),
            dma((32,)),
            dma((12,)),
            dma((16,)),
            dma((8,)),
        ],
        compiler_params=pltpu.CompilerParams(
            collective_id=0, has_side_effects=True, vmem_limit_bytes=56 << 20
        ),
        name="attention",
    )(q, k, v, mk, mv, req, info, w)


def tables(block_index):
    z = lax.axis_index("seq") // 8
    w = block_index.reshape(-1)
    holder = w // 64
    local = w - holder * 64
    owners = jnp.arange(16, dtype=jnp.int32)
    n = jnp.arange(32, dtype=jnp.int32)
    same = holder[:, None] == holder[None, :]
    count = jnp.sum(same.astype(jnp.int32), axis=1)
    place = jnp.sum((same & (n[None, :] < n[:, None])).astype(jnp.int32), axis=1)
    is_hot = count == TOPB
    rank = jnp.sum((same & (local[None, :] < local[:, None])).astype(jnp.int32), axis=1)
    lanes = jnp.arange(128, dtype=jnp.int32)
    mine = z * 2 + lax.axis_index("seq") % 2
    slot = jnp.where(is_hot, rank - 2 * mine, place)
    hit = (holder[:, None, None] == owners[None, :, None]) & (
        slot[:, None, None] == lanes[None, None, :]
    ) & (lanes < 2)[None, None, :]
    req = jnp.sum(jnp.where(hit, local[:, None, None], 0), axis=0)
    code = jnp.where(is_hot, 64 + rank, (z * 16 + holder) * 2 + place)
    at_code = n[:, None] == lanes[None, :]
    at_hot = is_hot[:, None] & ((rank + 32)[:, None] == lanes[None, :])
    at_owner = (is_hot & (rank == 0))[:, None] & (lanes == 40)[None, :]
    info = jnp.sum(
        jnp.where(at_code, code[:, None], 0)
        + jnp.where(at_hot, local[:, None], 0)
        + jnp.where(at_owner, holder[:, None], 0),
        axis=0,
    )
    return (
        jnp.broadcast_to(req[:, None, :], (16, 8, 128)),
        jnp.broadcast_to(info[None, :], (8, 128)),
    )


def shards(q, k, v, mk, mv, block_index, w):
    req, info = tables(block_index)
    return attention(
        q, k, v, mk.reshape(-1, BLOCK, 2 * HD), mv.reshape(-1, BLOCK, 2 * HD), req, info, w
    )


def solution(mesh):
    return jax.shard_map(
        shards,
        mesh=mesh,
        in_specs=(
            P("seq", "head"), P("seq", "head"), P("seq", "head"), P("seq", "head"),
            P("seq", "head"), P("seq", None), P("head", None),
        ),
        out_specs=P("seq", "head"),
        check_vma=False,
    )
```
